512 devices in a mesh: group: 16 (over x_hi, y, core), tensor: 32 (over x_lo, z).
Axes of the slice: x: 4 (x_hi: 2, x_lo: 2; x = x_hi * 2 + x_lo), y: 4, z: 16, core: 2. Of those that a mesh axis runs over, the one named last changes fastest.
Arguments:
- teacher_feat: bfloat16 [4096, 4096], P(('group', 'tensor')), may hold values from -6 to 6
- teacher_gain: float32 [4096], replicated, may hold values from 0.5 to 1.5
- teacher_proj: bfloat16 [4096, 256], P('tensor'), may hold values from -0.09375 to 0.09375
- teacher_proto: bfloat16 [256, 32768], P(None, 'tensor')
- center: float32 [32768], P('tensor'), may hold values from -3 to 3
- routes: int32 [256, 1], replicated, may hold values from 0 to 15; in each aligned block of 16 rows (0 to 15, 16 to 31, ...) at most 2 rows name the same one
- large_groups: int32 [1], replicated, may hold values from 1 to 15
- feat_large: bfloat16 [8192, 1024], P(('group', 'tensor')), may hold values from -6 to 6
- feat_huge: bfloat16 [8192, 1280], P(('group', 'tensor')), may hold values from -6 to 6
- gain_large: float32 [1024], replicated, may hold values from 0.5 to 1.5
- gain_huge: float32 [1280], replicated, may hold values from 0.5 to 1.5
- proj_large: bfloat16 [1024, 256], P('tensor'), may hold values from -0.1875 to 0.1875
- proj_huge: bfloat16 [1280, 256], P('tensor'), may hold values from -0.15625 to 0.15625
- proto_large: bfloat16 [256, 32768], P(None, 'tensor')
- proto_huge: bfloat16 [256, 32768], P(None, 'tensor')
Outputs:
- loss: float32 [1], replicated
- grad_large: bfloat16 [256, 32768], P(None, 'tensor')
- grad_huge: bfloat16 [256, 32768], P(None, 'tensor')
The draws below stay inside these ranges and needn't reach their ends.
Inputs may be any that keep to these rules, and one draw needn't show every extreme that they name: `routes`: of the 16 crops of one sending group, at most 2 name the same receiving group, and 2 is reached. `large_groups`: groups below this number train the large student, the rest the huge one.
All inputs are finite; a program needn't handle non-finite values.
Results may differ from the reference program's by a relative error of at most 0.012.
The reference program's roundings to bfloat16 on the way count: a program that leaves them out, or rounds other values in their place, can miss the bound.
Values may be sent and summed in bfloat16 or wider, within the bound.
No kernel may reach another device: no remote copies, remote signals or barrier semaphores. Data moves between devices by JAX's collectives and lax.ppermute only.
A program may use at most 64 MiB of HBM per device.

```python
import math
import jax
import jax.numpy as jnp
import numpy as np
from jax import lax

DT = 4096
DL = 1024
DH = 1280
B = 256
P_SIZE = 32768
PATCH = 16
CG = 16
CAP = 2
CROPS = 256
N_GROUP = 16


def prototype_weights(key, rows, cols, widest):
    normal_part = jax.random.normal(key, (rows, cols), jnp.float32) * (0.3 / math.sqrt(rows))
    column_scale = jnp.exp(jax.random.uniform(jax.random.fold_in(key, 7), (cols,), jnp.float32, 0.0, math.log(widest)))
    return (normal_part * column_scale[None, :]).astype(jnp.bfloat16)


def draw_teacher_proto(key, part):
    key = jax.random.fold_in(key, 11)
    return prototype_weights(key, B, P_SIZE, 1.0)


def draw_proto_large(key, part):
    key = jax.random.fold_in(key, 12)
    return prototype_weights(key, B, P_SIZE, 1.0)


def draw_proto_huge(key, part):
    key = jax.random.fold_in(key, 13)
    return prototype_weights(key, B, P_SIZE, 1.0)


def steps_of(key, shape, pieces, low, high):
    gain = 1.0
    for position, shards_of in pieces:
        steps = jax.random.uniform(jax.random.fold_in(jax.random.fold_in(key, 6), position), (shards_of,), jnp.float32, low / len(pieces), high / len(pieces))
        gain = gain * jnp.repeat(jnp.exp(steps), shape[position] // shards_of).reshape((-1,) + (1,) * (len(shape) - 1 - position))
    return gain


def deal_out(own_key, own, number, rows, amount, top, bound, slope):
    sequence = jax.random.permutation(own_key, amount)
    heavy_load, usual = portions_of(amount, rows * top, bound, slope, True), portions_of(amount, rows * top, bound, slope, False)
    places = jnp.arange(amount)

    def named(lengths, turn):
        used = int((lengths > 0).sum())
        fixed = max(1, used // 4)
        passed = fixed + (places - fixed + turn * (used - fixed)) % max(1, amount - fixed)
        return jnp.zeros((amount,), jnp.int32).at[sequence[jnp.where(places < fixed, places, passed)]].set(jnp.asarray(lengths, jnp.int32))

    lengths = jnp.where(number % 4 == 0, named(heavy_load, number // 4), named(usual, number - number // 4 - 1))
    mixed = jax.random.permutation(jax.random.fold_in(own, 3), amount)
    donor, sink = mixed[0:amount // 2 * 2:2], mixed[1:amount // 2 * 2:2]
    margin = jnp.minimum(lengths[donor] - 1, bound - lengths[sink]) // 2
    margin = jnp.where((donor == sequence[0]) | (sink == sequence[0]) | (lengths[sink] == 0), 0, jnp.maximum(margin, 0))
    passed = jax.random.randint(jax.random.fold_in(own, 4), (amount // 2,), 0, 1 << 20) % (margin + 1)
    lengths = lengths.at[donor].add(-passed).at[sink].add(passed)
    items = jnp.searchsorted(jnp.cumsum(lengths), jnp.arange(rows * top), side="right").astype(jnp.int32)
    table = items.reshape(top, rows).T
    table = table[jax.random.permutation(jax.random.fold_in(own, 1), rows)]
    turn = jax.random.randint(jax.random.fold_in(own, 2), (rows, 1), 0, top)
    return jnp.take_along_axis(table, (jnp.arange(top)[None, :] + turn) % top, axis=1)


def portions_of(count, total, limit, lean, full):
    loads = [(1 << 20) // math.isqrt(grade ** lean) + 1 for grade in range(1, count + 1)]
    largest = limit if full else min(limit, max(-(-total // count), total * loads[0] // sum(loads)))
    least = 1 if total - largest >= count - 1 else 0
    given, surplus = [largest] + [least] * (count - 1), total - largest - least * (count - 1)
    while surplus > 0:
        candidates = [i for i in range(1, count) if given[i] < largest] or [i for i in range(1, count) if given[i] < limit]
        mass, left = sum([loads[i] for i in candidates]), surplus
        for i in candidates:
            addition = min(limit - given[i], max(1, left * loads[i] // mass), surplus)
            given[i] = given[i] + addition
            surplus = surplus - addition
    return np.array(given)


def bell_draw(key, extent, scale, bound, shards=(), kind=jnp.bfloat16):
    factor_of = steps_of(key, extent, shards, -0.22, 0.18) if shards else 1.0
    entries = jax.random.normal(key, extent, jnp.float32) * scale * factor_of
    return jnp.minimum(jnp.maximum(entries, -bound), bound).astype(kind)


def setup_inputs(seed: int = 0) -> dict:
    splits = jax.random.split(jax.random.key(seed), 16)
    teacher_feat = bell_draw(splits[0], (CROPS * PATCH, DT), 1.0, 6.0, ((0, 512),))
    teacher_gain = jnp.clip(1.0 + 0.1 * jax.random.normal(splits[1], (DT,), jnp.float32), 0.5, 1.5)
    teacher_proj = bell_draw(splits[2], (DT, B), DT ** -0.5, 0.09375, ((0, 32),))
    teacher_proto = draw_teacher_proto(jax.random.fold_in(splits[15], 71), 0)
    center = bell_draw(splits[4], (P_SIZE,), 0.5, 3.0, ((0, 32),), jnp.float32)
    routes_keys = jax.random.split(jax.random.fold_in(splits[5], 1), CROPS // CG)
    routes_turns = jax.random.permutation(jax.random.fold_in(splits[5], 3), CROPS // CG)
    routes = jax.vmap(lambda own, number: deal_out(jax.random.fold_in(splits[5], 2), own, number, CG, N_GROUP, 1, CAP, 2))(routes_keys, routes_turns).reshape((CROPS, 1))
    large_groups = jax.random.randint(splits[6], (1,), 1, N_GROUP).astype(jnp.int32)
    feat_large = bell_draw(splits[7], (N_GROUP * N_GROUP * CAP * PATCH, DL), 1.0, 6.0, ((0, 512),))
    feat_huge = bell_draw(splits[8], (N_GROUP * N_GROUP * CAP * PATCH, DH), 1.0, 6.0, ((0, 512),))
    gain_large = jnp.clip(1.0 + 0.1 * jax.random.normal(splits[9], (DL,), jnp.float32), 0.5, 1.5)
    gain_huge = jnp.clip(1.0 + 0.1 * jax.random.normal(splits[10], (DH,), jnp.float32), 0.5, 1.5)
    proj_large = bell_draw(splits[11], (DL, B), DL ** -0.5, 0.1875, ((0, 32),))
    proj_huge = bell_draw(splits[12], (DH, B), DH ** -0.5, 0.15625, ((0, 32),))
    proto_large = draw_proto_large(jax.random.fold_in(splits[15], 71), 0)
    proto_huge = draw_proto_huge(jax.random.fold_in(splits[15], 71), 0)
    return {"teacher_feat": teacher_feat, "teacher_gain": teacher_gain, "teacher_proj": teacher_proj, "teacher_proto": teacher_proto, "center": center, "routes": routes, "large_groups": large_groups, "feat_large": feat_large, "feat_huge": feat_huge, "gain_large": gain_large, "gain_huge": gain_huge, "proj_large": proj_large, "proj_huge": proj_huge, "proto_large": proto_large, "proto_huge": proto_huge}


TEACHER_TEMP = 0.07
STUDENT_TEMP = 0.1
EPSILON = 1e-06

def layer_norm(values, gains):
    widened = values.astype(jnp.float32)
    row_mean = lax.optimization_barrier(jnp.mean(widened, axis=-1, keepdims=True))
    centred = widened - row_mean
    spread = lax.optimization_barrier(jnp.mean(centred * centred, axis=-1, keepdims=True))
    return (centred * lax.rsqrt(spread + EPSILON) * gains).astype(jnp.bfloat16)

def unit_rows(middle):
    return (middle * lax.rsqrt(lax.optimization_barrier(jnp.mean(middle * middle, axis=-1, keepdims=True)) + EPSILON)).astype(jnp.bfloat16)

def slot_table(routes):
    target_group = routes[:, 0].reshape(-1, CG).astype(jnp.int32)
    earlier = jnp.arange(CG)[:, None] > jnp.arange(CG)[None, :]
    matching = target_group[:, :, None] == target_group[:, None, :]
    slot_rank = lax.optimization_barrier(jnp.sum((matching & earlier).astype(jnp.int32), axis=2)).astype(jnp.int32)
    return (target_group, slot_rank)

def student_terms(blocks, slots, gains, weights, protos, wanted, mask):
    width = blocks.shape[2]
    normed = layer_norm(blocks[slots].reshape(-1, width), gains)
    units = unit_rows(jnp.dot(normed, weights, preferred_element_type=jnp.float32))
    scores = jnp.dot(units, protos, preferred_element_type=jnp.float32) / STUDENT_TEMP
    row_top = lax.optimization_barrier(jnp.max(scores, axis=-1, keepdims=True))
    row_total = lax.optimization_barrier(jnp.sum(jnp.exp(scores - row_top), axis=-1, keepdims=True))
    log_prob = scores - row_top - jnp.log(row_total)
    student_prob = jnp.exp(scores - row_top) / row_total
    cross = -jnp.sum(mask * wanted * log_prob)
    deltas = (mask * (student_prob - wanted) / STUDENT_TEMP).astype(jnp.bfloat16)
    head_grad = jnp.dot(units.T, deltas, preferred_element_type=jnp.float32)
    return (cross, head_grad)

def reference(teacher_feat, teacher_gain, teacher_proj, teacher_proto, center, routes, large_groups, feat_large, feat_huge, gain_large, gain_huge, proj_large, proj_huge, proto_large, proto_huge):
    target_group, slot_rank = slot_table(routes)
    groups = target_group.shape[0]
    source = jnp.broadcast_to(jnp.arange(groups, dtype=jnp.int32)[:, None], target_group.shape)
    slot_index = ((target_group * groups + source) * CAP + slot_rank).astype(jnp.int32)
    large_crop = (target_group < large_groups[0]).astype(jnp.int32)
    teacher_blocks = teacher_feat.reshape(groups, CG * PATCH, teacher_feat.shape[1])
    blocks_large = feat_large.reshape(-1, PATCH, feat_large.shape[1])
    blocks_huge = feat_huge.reshape(-1, PATCH, feat_huge.shape[1])

    def one_group(carry, inputs):
        loss_sum, total_large, total_huge = carry
        rows, slots, use_large = inputs
        teacher_unit = unit_rows(jnp.dot(layer_norm(rows, teacher_gain), teacher_proj, preferred_element_type=jnp.float32))
        logits = jnp.dot(teacher_unit, teacher_proto, preferred_element_type=jnp.float32)
        target = jax.nn.softmax((logits - center) / TEACHER_TEMP, axis=-1).astype(jnp.bfloat16)
        wanted = target.astype(jnp.float32)
        mask_large = jnp.repeat(use_large, PATCH).astype(jnp.float32)[:, None]
        mask_huge = 1.0 - mask_large
        cross_large, grad_large = student_terms(blocks_large, slots, gain_large, proj_large, proto_large, wanted, mask_large)
        cross_huge, grad_huge = student_terms(blocks_huge, slots, gain_huge, proj_huge, proto_huge, wanted, mask_huge)
        return ((loss_sum + cross_large + cross_huge, total_large + grad_large, total_huge + grad_huge), None)
    start = (jnp.zeros((), jnp.float32), jnp.zeros(proto_large.shape, jnp.float32), jnp.zeros(proto_huge.shape, jnp.float32))
    (loss_sum, grad_large, grad_huge), unused = lax.scan(one_group, start, (teacher_blocks, slot_index, large_crop))
    loss = loss_sum / (routes.shape[0] * PATCH)
    return (loss.reshape(1).astype(jnp.float32), (grad_large / PATCH).astype(jnp.bfloat16), (grad_huge / PATCH).astype(jnp.bfloat16))
```

```python
import jax
import jax.numpy as jnp
from jax import lax
from jax.sharding import PartitionSpec as P

PATCH = 16
CG = 16
NEAR = 4


TEACHER_TEMP = 0.07
STUDENT_TEMP = 0.1
EPSILON = 1e-06


def layer_norm(values, gains):
    widened = values.astype(jnp.float32)
    row_mean = jnp.mean(widened, axis=-1, keepdims=True)
    centred = widened - row_mean
    spread = jnp.mean(centred * centred, axis=-1, keepdims=True)
    return (centred * lax.rsqrt(spread + EPSILON) * gains).astype(jnp.bfloat16)


def unit_rows(middle):
    return (middle * lax.rsqrt(jnp.mean(middle * middle, axis=-1, keepdims=True) + EPSILON)).astype(
        jnp.bfloat16
    )


def gather_copies(values, axis):
    copies = jnp.broadcast_to(values[None], (lax.axis_size(axis), *values.shape))
    return lax.all_to_all(copies, axis, split_axis=0, concat_axis=0, tiled=True)


def shards(
    teacher_feat,
    teacher_gain,
    teacher_proj,
    teacher_proto,
    center,
    routes,
    large_groups,
    feat_large,
    feat_huge,
    gain_large,
    gain_huge,
    proj_large,
    proj_huge,
    proto_large,
    proto_huge,
):
    groups = lax.axis_size("group")
    tensors = lax.axis_size("tensor")
    own_group = lax.axis_index("group")
    own_tensor = lax.axis_index("tensor")
    protos = teacher_proto.shape[1]
    width = teacher_proto.shape[0]
    slots_per = tensors // groups
    far = tensors // NEAR
    own_near = own_tensor % NEAR
    far_groups = [[near + NEAR * other for other in range(far)] for near in range(NEAR)]

    weights = jnp.concatenate([teacher_proj, proj_large, proj_huge], axis=0)
    held = [weights] + [
        lax.ppermute(weights, "tensor", [(t, t ^ step) for t in range(tensors)])
        for step in range(1, NEAR)
    ]
    held = jnp.stack(held)
    ordered = [
        lax.dynamic_index_in_dim(held, own_near ^ place, 0, keepdims=False) for place in range(NEAR)
    ]
    first, second = teacher_proj.shape[0], proj_large.shape[0]
    teacher_w = jnp.concatenate([block[:first] for block in ordered], axis=0)
    large_w = jnp.concatenate([block[first : first + second] for block in ordered], axis=0)
    huge_w = jnp.concatenate([block[first + second :] for block in ordered], axis=0)

    is_large = own_group < large_groups[0]
    wide = feat_huge.shape[1]
    padded_large = jnp.pad(feat_large, ((0, 0), (0, wide - feat_large.shape[1])))
    student_feat = jnp.where(is_large, padded_large, feat_huge)
    swap = [
        ((j * groups + s) * slots_per + k, (s * groups + j) * slots_per + k)
        for j in range(groups)
        for s in range(groups)
        for k in range(slots_per)
    ]
    student_feat = lax.ppermute(student_feat, ("group", "tensor"), swap)
    teacher_normed = layer_norm(teacher_feat, teacher_gain)
    row_large = own_tensor // slots_per < large_groups[0]
    slim = feat_large.shape[1]
    normed_large = layer_norm(student_feat[:, :slim], gain_large).reshape(-1, far, slim // far)
    normed_large = jnp.pad(normed_large, ((0, 0), (0, 0), (0, (wide - slim) // far)))
    normed_huge = layer_norm(student_feat, gain_huge).reshape(-1, far, wide // far)
    student_normed = jnp.where(row_large, normed_large, normed_huge)

    teacher_cols = lax.all_to_all(
        teacher_normed.reshape(-1, far, teacher_normed.shape[1] // far).transpose(1, 0, 2),
        "tensor",
        split_axis=0,
        concat_axis=0,
        tiled=True,
        axis_index_groups=far_groups,
    )
    student_cols = lax.all_to_all(
        student_normed.transpose(1, 0, 2),
        "tensor",
        split_axis=0,
        concat_axis=0,
        tiled=True,
        axis_index_groups=far_groups,
    )
    far_large = (
        (jnp.arange(far, dtype=jnp.int32) * NEAR + own_near) // slots_per < large_groups[0]
    )[:, None, None]
    zero = jnp.zeros((), jnp.bfloat16)
    part_teacher = jnp.einsum(
        "crf,fb->crb", teacher_cols, teacher_w, preferred_element_type=jnp.float32
    )
    part_student = jnp.einsum(
        "crf,fb->crb",
        jnp.where(far_large, student_cols[:, :, : large_w.shape[0]], zero),
        large_w,
        preferred_element_type=jnp.float32,
    ) + jnp.einsum(
        "crf,fb->crb",
        jnp.where(far_large, zero, student_cols),
        huge_w,
        preferred_element_type=jnp.float32,
    )
    parts = lax.all_to_all(
        jnp.concatenate([part_teacher, part_student], axis=1),
        "tensor",
        split_axis=0,
        concat_axis=0,
        tiled=True,
        axis_index_groups=far_groups,
    )
    units = gather_copies(unit_rows(jnp.sum(parts, axis=0)), "tensor")
    teacher_rows = teacher_feat.shape[0]
    teacher_units = units[:, :teacher_rows].reshape(-1, width)
    slot_units = units[:, teacher_rows:].reshape(-1, width)

    target_group = lax.dynamic_index_in_dim(
        routes[:, 0].reshape(-1, CG), own_group, 0, keepdims=False
    )
    earlier = jnp.arange(CG)[:, None] > jnp.arange(CG)[None, :]
    matching = target_group[:, None] == target_group[None, :]
    slot_rank = jnp.sum((matching & earlier).astype(jnp.int32), axis=1)
    crop_slot = target_group * slots_per + slot_rank
    row_slot = (crop_slot[:, None] * PATCH + jnp.arange(PATCH, dtype=jnp.int32)[None, :]).reshape(
        -1
    )
    crop_large = jnp.repeat(target_group < large_groups[0], PATCH)[:, None]
    chosen = (row_slot[:, None] == jnp.arange(slot_units.shape[0])[None, :]).astype(jnp.bfloat16)
    student_units = jnp.dot(chosen, slot_units, preferred_element_type=jnp.float32).astype(
        jnp.bfloat16
    )
    both_units = jnp.concatenate(
        [jnp.where(crop_large, student_units, zero), jnp.where(crop_large, zero, student_units)],
        axis=1,
    )
    both_protos = jnp.concatenate([proto_large, proto_huge], axis=0)
    shifted = (
        jnp.dot(teacher_units, teacher_proto, preferred_element_type=jnp.float32) - center[None, :]
    ) / TEACHER_TEMP
    scores = jnp.dot(both_units, both_protos, preferred_element_type=jnp.float32) / STUDENT_TEMP

    teacher_top = jnp.max(shifted, axis=1)
    teacher_exp = jnp.exp(shifted - teacher_top[:, None])
    student_top = jnp.max(scores, axis=1)
    student_exp = jnp.exp(scores - student_top[:, None])
    stats = jnp.stack(
        [
            teacher_top,
            jnp.sum(teacher_exp, axis=1),
            jnp.sum(teacher_exp * scores, axis=1),
            student_top,
            jnp.sum(student_exp, axis=1),
        ]
    )
    stats = gather_copies(stats, "tensor")
    top_t = jnp.max(stats[:, 0], axis=0)
    scale_t = jnp.exp(stats[:, 0] - top_t[None, :])
    total_t = jnp.sum(stats[:, 1] * scale_t, axis=0)
    crossed = jnp.sum(stats[:, 2] * scale_t, axis=0)
    top_s = jnp.max(stats[:, 3], axis=0)
    total_s = jnp.sum(stats[:, 4] * jnp.exp(stats[:, 3] - top_s[None, :]), axis=0)
    group_loss = jnp.sum(top_s + jnp.log(total_s) - crossed / total_t)
    target = (jnp.exp(shifted - top_t[:, None]) / total_t[:, None]).astype(jnp.bfloat16)
    student_prob = jnp.exp(scores - top_s[:, None]) / total_s[:, None]
    deltas = ((student_prob - target.astype(jnp.float32)) / STUDENT_TEMP).astype(jnp.bfloat16)
    grads = lax.dot_general(
        both_units, deltas, (((0,), (0,)), ((), ())), preferred_element_type=jnp.float32
    )

    high = group_loss.astype(jnp.bfloat16)
    rest = group_loss - high.astype(jnp.float32)
    middle = rest.astype(jnp.bfloat16)
    low = (rest - middle.astype(jnp.float32)).astype(jnp.bfloat16)
    lane = jnp.arange(128)
    note = jnp.where(lane == 0, high, jnp.where(lane == 1, middle, jnp.where(lane == 2, low, zero)))
    grad_rows = grads.shape[0] // groups
    sent = jnp.concatenate(
        [
            grads.astype(jnp.bfloat16).reshape(groups, grad_rows, protos),
            jnp.broadcast_to(note, (groups, grad_rows, 128)),
        ],
        axis=2,
    )
    taken = lax.all_to_all(sent, "group", split_axis=0, concat_axis=0, tiled=True)
    loss = (
        jnp.sum(taken[:, 0, protos : protos + 3].astype(jnp.float32)) / (routes.shape[0] * PATCH)
    ).reshape(1)
    summed = jnp.sum(taken[:, :, :protos].astype(jnp.float32), axis=0) / PATCH
    whole = gather_copies(summed.astype(jnp.bfloat16), "group").reshape(-1, protos)
    return (loss, whole[:width], whole[width:])


def solution(mesh):
    placed = (
        P(("group", "tensor"), None),
        P(),
        P("tensor", None),
        P(None, "tensor"),
        P("tensor"),
        P(),
        P(),
        P(("group", "tensor"), None),
        P(("group", "tensor"), None),
        P(),
        P(),
        P("tensor", None),
        P("tensor", None),
        P(None, "tensor"),
        P(None, "tensor"),
    )
    return jax.shard_map(
        shards,
        mesh=mesh,
        in_specs=placed,
        out_specs=(P(), P(None, "tensor"), P(None, "tensor")),
        check_vma=False,
    )
```

```python
import jax
import jax.numpy as jnp
from jax import lax
from jax.sharding import PartitionSpec as P

PATCH = 16
CG = 16
NEAR = 4


TEACHER_TEMP = 0.07
STUDENT_TEMP = 0.1
EPSILON = 1e-06


def layer_norm(values, gains):
    widened = values.astype(jnp.float32)
    row_mean = jnp.mean(widened, axis=-1, keepdims=True)
    centred = widened - row_mean
    spread = jnp.mean(centred * centred, axis=-1, keepdims=True)
    return (centred * lax.rsqrt(spread + EPSILON) * gains).astype(jnp.bfloat16)


def unit_rows(middle):
    return (middle * lax.rsqrt(jnp.mean(middle * middle, axis=-1, keepdims=True) + EPSILON)).astype(
        jnp.bfloat16
    )


def gather_copies(values, axis):
    copies = jnp.broadcast_to(values[None], (lax.axis_size(axis), *values.shape))
    return lax.all_to_all(copies, axis, split_axis=0, concat_axis=0, tiled=True)


def log_total(logs):
    top = jnp.max(logs, axis=0)
    return top + jnp.log(jnp.sum(jnp.exp(logs - top[None, :]), axis=0))


def parts_of(value):
    high = lax.reduce_precision(value, 8, 7)
    middle = lax.reduce_precision(value - high, 8, 7)
    low = lax.reduce_precision(value - high - middle, 8, 7)
    lane = jnp.arange(128)
    zero = jnp.zeros((), jnp.float32)
    parts = jnp.where(lane == 0, high, jnp.where(lane == 1, middle, jnp.where(lane == 2, low, zero)))
    return parts.astype(jnp.bfloat16)[None, :]


def partial_grad(units, deltas):
    return lax.dot_general(
        units, deltas, (((0,), (0,)), ((), ())), preferred_element_type=jnp.float32
    )


def shards(
    teacher_feat,
    teacher_gain,
    teacher_proj,
    teacher_proto,
    center,
    routes,
    large_groups,
    feat_large,
    feat_huge,
    gain_large,
    gain_huge,
    proj_large,
    proj_huge,
    proto_large,
    proto_huge,
):
    groups = lax.axis_size("group")
    tensors = lax.axis_size("tensor")
    own_group = lax.axis_index("group")
    own_tensor = lax.axis_index("tensor")
    protos = teacher_proto.shape[1]
    width = teacher_proto.shape[0]
    slots_per = tensors // groups
    far = tensors // NEAR
    own_near = own_tensor % NEAR
    far_groups = [[near + NEAR * other for other in range(far)] for near in range(NEAR)]

    is_large = own_group < large_groups[0]
    wide = feat_huge.shape[1]
    padded_large = jnp.pad(feat_large, ((0, 0), (0, wide - feat_large.shape[1])))
    student_feat = jnp.where(is_large, padded_large, feat_huge)
    student_feat, teacher_proj = lax.optimization_barrier((student_feat, teacher_proj))
    swap = [
        ((j * groups + s) * slots_per + k, (s * groups + j) * slots_per + k)
        for j in range(groups)
        for s in range(groups)
        for k in range(slots_per)
    ]
    student_feat = lax.ppermute(student_feat, ("group", "tensor"), swap)
    teacher_normed = layer_norm(teacher_feat, teacher_gain)
    row_large = own_tensor // slots_per < large_groups[0]
    slim = feat_large.shape[1]
    normed_large = layer_norm(student_feat[:, :slim], gain_large).reshape(-1, far, slim // far)
    normed_large = jnp.pad(normed_large, ((0, 0), (0, 0), (0, (wide - slim) // far)))
    normed_huge = layer_norm(student_feat, gain_huge).reshape(-1, far, wide // far)
    student_normed = jnp.where(row_large, normed_large, normed_huge)

    weights = jnp.concatenate([teacher_proj, proj_large, proj_huge], axis=0)
    held = [weights] + [
        lax.ppermute(weights, "tensor", [(t, t ^ step) for t in range(tensors)])
        for step in range(1, NEAR)
    ]
    held = jnp.stack(held)
    ordered = [
        lax.dynamic_index_in_dim(held, own_near ^ place, 0, keepdims=False) for place in range(NEAR)
    ]
    first, second = teacher_proj.shape[0], proj_large.shape[0]
    teacher_w = jnp.concatenate([block[:first] for block in ordered], axis=0)
    large_w = jnp.concatenate([block[first : first + second] for block in ordered], axis=0)
    huge_w = jnp.concatenate([block[first + second :] for block in ordered], axis=0)

    teacher_rows = teacher_feat.shape[0]
    piece = teacher_feat.shape[1] // far
    slot_pad = piece // 2 - wide // far
    teacher_sent = teacher_normed.reshape(teacher_rows, far, piece).transpose(1, 0, 2)
    student_sent = jnp.pad(student_normed, ((0, 0), (0, 0), (0, slot_pad))).transpose(1, 0, 2)
    half = student_sent.shape[1] // 2
    student_sent = jnp.concatenate([student_sent[:, :half], student_sent[:, half:]], axis=2)
    cols = lax.all_to_all(
        jnp.concatenate([teacher_sent, student_sent], axis=1),
        "tensor",
        split_axis=0,
        concat_axis=0,
        tiled=True,
        axis_index_groups=far_groups,
    )
    teacher_cols = cols[:, :teacher_rows]
    student_cols = jnp.concatenate(
        [
            cols[:, teacher_rows:, : wide // far],
            cols[:, teacher_rows:, piece // 2 : piece // 2 + wide // far],
        ],
        axis=1,
    )
    far_large = (
        (jnp.arange(far, dtype=jnp.int32) * NEAR + own_near) // slots_per < large_groups[0]
    )[:, None, None]
    zero = jnp.zeros((), jnp.bfloat16)
    part_teacher = jnp.einsum(
        "crf,fb->crb", teacher_cols, teacher_w, preferred_element_type=jnp.float32
    )
    part_student = jnp.einsum(
        "crf,fb->crb",
        jnp.where(far_large, student_cols[:, :, : large_w.shape[0]], zero),
        large_w,
        preferred_element_type=jnp.float32,
    ) + jnp.einsum(
        "crf,fb->crb",
        jnp.where(far_large, zero, student_cols),
        huge_w,
        preferred_element_type=jnp.float32,
    )
    parts = lax.all_to_all(
        jnp.concatenate([part_teacher, part_student], axis=1),
        "tensor",
        split_axis=0,
        concat_axis=0,
        tiled=True,
        axis_index_groups=far_groups,
    )
    units = gather_copies(unit_rows(jnp.sum(parts, axis=0)), "tensor")
    teacher_units = units[:, :teacher_rows].reshape(-1, width)
    slot_units = units[:, teacher_rows:].reshape(-1, width)

    target_group = lax.dynamic_index_in_dim(
        routes[:, 0].reshape(-1, CG), own_group, 0, keepdims=False
    )
    earlier = jnp.arange(CG)[:, None] > jnp.arange(CG)[None, :]
    matching = target_group[:, None] == target_group[None, :]
    slot_rank = jnp.sum((matching & earlier).astype(jnp.int32), axis=1)
    crop_slot = target_group * slots_per + slot_rank
    row_slot = (crop_slot[:, None] * PATCH + jnp.arange(PATCH, dtype=jnp.int32)[None, :]).reshape(
        -1
    )
    crop_large = jnp.repeat(target_group < large_groups[0], PATCH)[:, None]
    chosen = (row_slot[:, None] == jnp.arange(slot_units.shape[0])[None, :]).astype(jnp.bfloat16)
    student_units = jnp.dot(chosen, slot_units, preferred_element_type=jnp.float32).astype(
        jnp.bfloat16
    )
    both_units = jnp.concatenate(
        [jnp.where(crop_large, student_units, zero), jnp.where(crop_large, zero, student_units)],
        axis=1,
    )
    both_protos = jnp.concatenate([proto_large, proto_huge], axis=0)
    shifted = (
        jnp.dot(teacher_units, teacher_proto, preferred_element_type=jnp.float32) - center[None, :]
    ) / TEACHER_TEMP
    scores = jnp.dot(both_units, both_protos, preferred_element_type=jnp.float32) / STUDENT_TEMP

    teacher_top = jnp.max(shifted, axis=1)
    teacher_exp = jnp.exp(shifted - teacher_top[:, None])
    teacher_sum = jnp.sum(teacher_exp, axis=1)
    student_top = jnp.max(scores, axis=1)
    student_sum = jnp.sum(jnp.exp(scores - student_top[:, None]), axis=1)
    stats = jnp.stack(
        [
            teacher_top + jnp.log(teacher_sum),
            jnp.sum(teacher_exp * scores, axis=1) / teacher_sum,
            student_top + jnp.log(student_sum),
        ]
    )
    stats = gather_copies(stats.reshape(-1, 128), "tensor").reshape(tensors, 3, -1)
    log_t = log_total(stats[:, 0])
    crossed = jnp.sum(stats[:, 1] * jnp.exp(stats[:, 0] - log_t[None, :]), axis=0)
    log_s = log_total(stats[:, 2])
    group_loss = jnp.sum(log_s - crossed)
    target = lax.reduce_precision(jnp.exp(shifted - log_t[:, None]), 8, 7)
    student_prob = jnp.exp(scores - log_s[:, None])
    deltas = ((student_prob - target) / STUDENT_TEMP).astype(jnp.bfloat16)

    own_core = own_group % 2
    kept_rows = crop_large == (own_core == 0)
    gives = partial_grad(jnp.where(kept_rows, zero, student_units), deltas)
    keeps = partial_grad(jnp.where(kept_rows, student_units, zero), deltas)
    pairs = [(g, g ^ 1) for g in range(groups)]
    got = lax.ppermute(
        jnp.concatenate(
            [gives.astype(jnp.bfloat16), jnp.broadcast_to(parts_of(group_loss), (width, 128))],
            axis=1,
        ),
        "group",
        pairs,
    )
    chip_grad = keeps + got[:, :protos].astype(jnp.float32)
    chip_loss = group_loss + jnp.sum(got[0, protos:].astype(jnp.float32))
    chips = groups // 2
    grad_rows = width // chips
    sent = jnp.concatenate(
        [chip_grad.astype(jnp.bfloat16), jnp.broadcast_to(parts_of(chip_loss), (width, 128))],
        axis=1,
    ).reshape(chips, grad_rows, protos + 128)
    same_core = [[core + 2 * chip for chip in range(chips)] for core in range(2)]
    taken = lax.all_to_all(
        sent, "group", split_axis=0, concat_axis=0, tiled=True, axis_index_groups=same_core
    )
    loss = (
        jnp.sum(taken[:, 0, protos:].astype(jnp.float32)) / (routes.shape[0] * PATCH)
    ).reshape(1)
    summed = jnp.sum(taken[:, :, :protos].astype(jnp.float32), axis=0) / PATCH
    mine = lax.all_to_all(
        jnp.broadcast_to(summed.astype(jnp.bfloat16)[None], (chips, grad_rows, protos)),
        "group",
        split_axis=0,
        concat_axis=0,
        tiled=True,
        axis_index_groups=same_core,
    ).reshape(width, protos)
    other = lax.ppermute(mine, "group", pairs)
    return (
        loss,
        jnp.where(own_core == 0, mine, other),
        jnp.where(own_core == 0, other, mine),
    )


def solution(mesh):
    placed = (
        P(("group", "tensor"), None),
        P(),
        P("tensor", None),
        P(None, "tensor"),
        P("tensor"),
        P(),
        P(),
        P(("group", "tensor"), None),
        P(("group", "tensor"), None),
        P(),
        P(),
        P("tensor", None),
        P("tensor", None),
        P(None, "tensor"),
        P(None, "tensor"),
    )
    return jax.shard_map(
        shards,
        mesh=mesh,
        in_specs=placed,
        out_specs=(P(), P(None, "tensor"), P(None, "tensor")),
        check_vma=False,
    )
```

```python
import jax
import jax.numpy as jnp
from jax import lax
from jax.sharding import PartitionSpec as P

PATCH = 16
CG = 16
NEAR = 4


TEACHER_TEMP = 0.07
STUDENT_TEMP = 0.1
EPSILON = 1e-06


def layer_norm(values, gains):
    widened = values.astype(jnp.float32)
    row_mean = jnp.mean(widened, axis=-1, keepdims=True)
    centred = widened - row_mean
    spread = jnp.mean(centred * centred, axis=-1, keepdims=True)
    return (centred * lax.rsqrt(spread + EPSILON) * gains).astype(jnp.bfloat16)


def unit_rows(middle):
    return (middle * lax.rsqrt(jnp.mean(middle * middle, axis=-1, keepdims=True) + EPSILON)).astype(
        jnp.bfloat16
    )


def gather_copies(values, axis):
    copies = jnp.broadcast_to(values[None], (lax.axis_size(axis), *values.shape))
    return lax.all_to_all(copies, axis, split_axis=0, concat_axis=0, tiled=True)


def log_total(logs):
    top = jnp.max(logs, axis=0)
    return top + jnp.log(jnp.sum(jnp.exp(logs - top[None, :]), axis=0))


def parts_of(values):
    high = lax.reduce_precision(values, 8, 7)
    middle = lax.reduce_precision(values - high, 8, 7)
    low = lax.reduce_precision(values - high - middle, 8, 7)
    return jnp.stack([high, middle, low]).astype(jnp.bfloat16)


def crop_rows(routes, group, large, slots_per):
    target_group = lax.dynamic_index_in_dim(routes[:, 0].reshape(-1, CG), group, 0, keepdims=False)
    earlier = jnp.arange(CG)[:, None] > jnp.arange(CG)[None, :]
    matching = target_group[:, None] == target_group[None, :]
    slot_rank = jnp.sum((matching & earlier).astype(jnp.int32), axis=1)
    first_row = (target_group * slots_per + slot_rank) * PATCH
    row_slot = (first_row[:, None] + jnp.arange(PATCH, dtype=jnp.int32)[None, :]).reshape(-1)
    return (row_slot, jnp.repeat(target_group < large, PATCH)[:, None])


def partial_grad(units, deltas):
    return lax.dot_general(
        units, deltas, (((0,), (0,)), ((), ())), preferred_element_type=jnp.float32
    )


def shards(
    teacher_feat,
    teacher_gain,
    teacher_proj,
    teacher_proto,
    center,
    routes,
    large_groups,
    feat_large,
    feat_huge,
    gain_large,
    gain_huge,
    proj_large,
    proj_huge,
    proto_large,
    proto_huge,
):
    groups = lax.axis_size("group")
    tensors = lax.axis_size("tensor")
    own_group = lax.axis_index("group")
    own_tensor = lax.axis_index("tensor")
    protos = teacher_proto.shape[1]
    width = teacher_proto.shape[0]
    slots_per = tensors // groups
    far = tensors // NEAR
    own_near = own_tensor % NEAR
    far_groups = [[near + NEAR * other for other in range(far)] for near in range(NEAR)]

    is_large = own_group < large_groups[0]
    wide = feat_huge.shape[1]
    padded_large = jnp.pad(feat_large, ((0, 0), (0, wide - feat_large.shape[1])))
    student_feat = jnp.where(is_large, padded_large, feat_huge)
    swap = [
        ((j * groups + s) * slots_per + k, (s * groups + j) * slots_per + k)
        for j in range(groups)
        for s in range(groups)
        for k in range(slots_per)
    ]
    student_feat = lax.ppermute(student_feat, ("group", "tensor"), swap)
    teacher_normed = layer_norm(teacher_feat, teacher_gain)
    teacher_normed, teacher_proj = lax.optimization_barrier((teacher_normed, teacher_proj))
    row_large = own_tensor // slots_per < large_groups[0]
    slim = feat_large.shape[1]
    normed_large = layer_norm(student_feat[:, :slim], gain_large).reshape(-1, far, slim // far)
    normed_large = jnp.pad(normed_large, ((0, 0), (0, 0), (0, (wide - slim) // far)))
    normed_huge = layer_norm(student_feat, gain_huge).reshape(-1, far, wide // far)
    student_normed = jnp.where(row_large, normed_large, normed_huge)

    weights = jnp.concatenate([teacher_proj, proj_large, proj_huge], axis=0)
    held = [weights] + [
        lax.ppermute(weights, "tensor", [(t, t ^ step) for t in range(tensors)])
        for step in range(1, NEAR)
    ]
    teacher_rows = teacher_feat.shape[0]
    piece = teacher_feat.shape[1] // far
    slot_pad = piece // 2 - wide // far
    teacher_sent = teacher_normed.reshape(teacher_rows, far, piece).transpose(1, 0, 2)
    student_sent = jnp.pad(student_normed, ((0, 0), (0, 0), (0, slot_pad))).transpose(1, 0, 2)
    half = student_sent.shape[1] // 2
    student_sent = jnp.concatenate([student_sent[:, :half], student_sent[:, half:]], axis=2)
    cols = lax.all_to_all(
        jnp.concatenate([teacher_sent, student_sent], axis=1),
        "tensor",
        split_axis=0,
        concat_axis=0,
        tiled=True,
        axis_index_groups=far_groups,
    )
    cols, held = lax.optimization_barrier((cols, held))
    held = jnp.stack(held)
    ordered = [
        lax.dynamic_index_in_dim(held, own_near ^ place, 0, keepdims=False) for place in range(NEAR)
    ]
    first, second = teacher_proj.shape[0], proj_large.shape[0]
    teacher_w = jnp.concatenate([block[:first] for block in ordered], axis=0)
    large_w = jnp.concatenate([block[first : first + second] for block in ordered], axis=0)
    huge_w = jnp.concatenate([block[first + second :] for block in ordered], axis=0)
    teacher_cols = cols[:, :teacher_rows]
    student_cols = jnp.concatenate(
        [
            cols[:, teacher_rows:, : wide // far],
            cols[:, teacher_rows:, piece // 2 : piece // 2 + wide // far],
        ],
        axis=1,
    )
    far_large = (
        (jnp.arange(far, dtype=jnp.int32) * NEAR + own_near) // slots_per < large_groups[0]
    )[:, None, None]
    zero = jnp.zeros((), jnp.bfloat16)
    part_teacher = jnp.einsum(
        "crf,fb->crb", teacher_cols, teacher_w, preferred_element_type=jnp.float32
    )
    part_student = jnp.einsum(
        "crf,fb->crb",
        jnp.where(far_large, student_cols[:, :, : large_w.shape[0]], zero),
        large_w,
        preferred_element_type=jnp.float32,
    ) + jnp.einsum(
        "crf,fb->crb",
        jnp.where(far_large, zero, student_cols),
        huge_w,
        preferred_element_type=jnp.float32,
    )
    own_core = own_group % 2
    row_slot, crop_large = crop_rows(routes, own_group, large_groups[0], slots_per)
    _, other_large = crop_rows(routes, own_group ^ 1, large_groups[0], slots_per)
    chosen = (
        row_slot[:, None] == jnp.arange(tensors * PATCH, dtype=jnp.int32)[None, :]
    ).astype(jnp.bfloat16)
    kept_rows = crop_large == (own_core == 0)
    other_rows = other_large == (own_core == 0)

    parts = lax.all_to_all(
        jnp.concatenate([part_teacher, part_student], axis=1),
        "tensor",
        split_axis=0,
        concat_axis=0,
        tiled=True,
        axis_index_groups=far_groups,
    )
    units = unit_rows(jnp.sum(parts, axis=0))
    units, chosen, crop_large, kept_rows, other_rows = lax.optimization_barrier(
        (units, chosen, crop_large, kept_rows, other_rows)
    )
    units = gather_copies(units, "tensor")
    teacher_units = units[:, :teacher_rows].reshape(-1, width)
    slot_units = units[:, teacher_rows:].reshape(-1, width)

    student_units = jnp.dot(chosen, slot_units, preferred_element_type=jnp.float32).astype(
        jnp.bfloat16
    )
    both_units = jnp.concatenate(
        [jnp.where(crop_large, student_units, zero), jnp.where(crop_large, zero, student_units)],
        axis=1,
    )
    both_protos = jnp.concatenate([proto_large, proto_huge], axis=0)
    shifted = (
        jnp.dot(teacher_units, teacher_proto, preferred_element_type=jnp.float32) - center[None, :]
    ) / TEACHER_TEMP
    scores = jnp.dot(both_units, both_protos, preferred_element_type=jnp.float32) / STUDENT_TEMP

    teacher_top = jnp.max(shifted, axis=1)
    teacher_exp = jnp.exp(shifted - teacher_top[:, None])
    teacher_sum = jnp.sum(teacher_exp, axis=1)
    student_top = jnp.max(scores, axis=1)
    student_sum = jnp.sum(jnp.exp(scores - student_top[:, None]), axis=1)
    stats = jnp.stack(
        [
            teacher_top + jnp.log(teacher_sum),
            jnp.sum(teacher_exp * scores, axis=1) / teacher_sum,
            student_top + jnp.log(student_sum),
        ]
    )
    stats = gather_copies(stats.reshape(-1, 128), "tensor").reshape(tensors, 3, -1)
    log_t = log_total(stats[:, 0])
    crossed = jnp.sum(stats[:, 1] * jnp.exp(stats[:, 0] - log_t[None, :]), axis=0)
    log_s = log_total(stats[:, 2])
    group_loss = jnp.sum((log_s - crossed).reshape(-1, 128), axis=0)
    target = lax.reduce_precision(jnp.exp(shifted - log_t[:, None]), 8, 7)
    student_prob = jnp.exp(scores - log_s[:, None])
    deltas = ((student_prob - target) / STUDENT_TEMP).astype(jnp.bfloat16)

    pairs = [(g, g ^ 1) for g in range(groups)]
    rows = deltas.shape[0]
    note = jnp.pad(parts_of(group_loss), ((0, PATCH - 3), (0, protos + width - 128)))
    got = lax.ppermute(
        jnp.concatenate([jnp.concatenate([deltas, student_units], axis=1), note], axis=0),
        "group",
        pairs,
    )
    chip_grad = partial_grad(jnp.where(kept_rows, student_units, zero), deltas) + partial_grad(
        jnp.where(other_rows, got[:rows, protos:], zero), got[:rows, :protos]
    )
    chip_loss = group_loss + jnp.sum(got[rows : rows + 3, :128].astype(jnp.float32), axis=0)
    chips = groups // 2
    grad_rows = width // chips
    note = jnp.pad(parts_of(chip_loss), ((0, grad_rows - 3), (0, 0)))
    sent = jnp.concatenate(
        [
            chip_grad.astype(jnp.bfloat16).reshape(chips, grad_rows, protos),
            jnp.broadcast_to(note[None], (chips, grad_rows, 128)),
        ],
        axis=2,
    )
    same_core = [[core + 2 * chip for chip in range(chips)] for core in range(2)]
    taken = lax.all_to_all(
        sent, "group", split_axis=0, concat_axis=0, tiled=True, axis_index_groups=same_core
    )
    loss = (
        jnp.sum(taken[:, :3, protos:].astype(jnp.float32)) / (routes.shape[0] * PATCH)
    ).reshape(1)
    summed = jnp.sum(taken[:, :, :protos].astype(jnp.float32), axis=0) / PATCH
    mine = lax.all_to_all(
        jnp.broadcast_to(summed.astype(jnp.bfloat16)[None], (chips, grad_rows, protos)),
        "group",
        split_axis=0,
        concat_axis=0,
        tiled=True,
        axis_index_groups=same_core,
    ).reshape(width, protos)
    other = lax.ppermute(mine, "group", pairs)
    return (
        loss,
        jnp.where(own_core == 0, mine, other),
        jnp.where(own_core == 0, other, mine),
    )


def solution(mesh):
    placed = (
        P(("group", "tensor"), None),
        P(),
        P("tensor", None),
        P(None, "tensor"),
        P("tensor"),
        P(),
        P(),
        P(("group", "tensor"), None),
        P(("group", "tensor"), None),
        P(),
        P(),
        P("tensor", None),
        P("tensor", None),
        P(None, "tensor"),
        P(None, "tensor"),
    )
    return jax.shard_map(
        shards,
        mesh=mesh,
        in_specs=placed,
        out_specs=(P(), P(None, "tensor"), P(None, "tensor")),
        check_vma=False,
    )
```

```python
import jax
import jax.numpy as jnp
from jax import lax
from jax.sharding import PartitionSpec as P

PATCH = 16
CG = 16
FAR = 4


TEACHER_TEMP = 0.07
STUDENT_TEMP = 0.1
EPSILON = 1e-06


def layer_norm(values, gains):
    widened = values.astype(jnp.float32)
    row_mean = jnp.mean(widened, axis=-1, keepdims=True)
    centred = widened - row_mean
    spread = jnp.mean(centred * centred, axis=-1, keepdims=True)
    return (centred * lax.rsqrt(spread + EPSILON) * gains).astype(jnp.bfloat16)


def unit_rows(middle):
    return (middle * lax.rsqrt(jnp.mean(middle * middle, axis=-1, keepdims=True) + EPSILON)).astype(
        jnp.bfloat16
    )


def gather_copies(values, axis):
    copies = jnp.broadcast_to(values[None], (lax.axis_size(axis), *values.shape))
    return lax.all_to_all(copies, axis, split_axis=0, concat_axis=0, tiled=True)


def log_total(logs):
    top = jnp.max(logs, axis=0)
    return top + jnp.log(jnp.sum(jnp.exp(logs - top[None, :]), axis=0))


def by_near(columns, halves):
    rows, tensors, wide = columns.shape
    columns = columns.reshape(rows, halves, FAR, FAR, wide).transpose(1, 3, 0, 2, 4)
    return columns.reshape(tensors // FAR, rows, FAR * wide)


def parts_of(values):
    high = lax.reduce_precision(values, 8, 7)
    middle = lax.reduce_precision(values - high, 8, 7)
    low = lax.reduce_precision(values - high - middle, 8, 7)
    return jnp.stack([high, middle, low]).astype(jnp.bfloat16)


def crop_rows(routes, group, large, slots_per):
    target_group = lax.dynamic_index_in_dim(routes[:, 0].reshape(-1, CG), group, 0, keepdims=False)
    earlier = jnp.arange(CG)[:, None] > jnp.arange(CG)[None, :]
    matching = target_group[:, None] == target_group[None, :]
    slot_rank = jnp.sum((matching & earlier).astype(jnp.int32), axis=1)
    first_row = (target_group * slots_per + slot_rank) * PATCH
    row_slot = (first_row[:, None] + jnp.arange(PATCH, dtype=jnp.int32)[None, :]).reshape(-1)
    return (row_slot, jnp.repeat(target_group < large, PATCH)[:, None])


def partial_grad(units, deltas):
    return lax.dot_general(
        units, deltas, (((0,), (0,)), ((), ())), preferred_element_type=jnp.float32
    )


def alone(values, live, exchange):
    values, live = lax.optimization_barrier((values, live))
    return lax.optimization_barrier((exchange(values), live))


def shards(
    teacher_feat,
    teacher_gain,
    teacher_proj,
    teacher_proto,
    center,
    routes,
    large_groups,
    feat_large,
    feat_huge,
    gain_large,
    gain_huge,
    proj_large,
    proj_huge,
    proto_large,
    proto_huge,
):
    groups = lax.axis_size("group")
    tensors = lax.axis_size("tensor")
    own_group = lax.axis_index("group")
    own_tensor = lax.axis_index("tensor")
    protos = teacher_proto.shape[1]
    width = teacher_proto.shape[0]
    slots_per = tensors // groups
    near = tensors // FAR
    halves = tensors // (FAR * FAR)
    own_far = own_tensor // FAR % FAR
    own_core = own_group % 2
    near_groups = [
        [half * FAR * FAR + place * FAR + low for half in range(halves) for low in range(FAR)]
        for place in range(FAR)
    ]
    far_groups = [
        [half * FAR * FAR + place * FAR + low for place in range(FAR)]
        for half in range(halves)
        for low in range(FAR)
    ]
    pairs = [(g, g ^ 1) for g in range(groups)]

    is_large = own_group < large_groups[0]
    wide = feat_huge.shape[1]
    padded_large = jnp.pad(feat_large, ((0, 0), (0, wide - feat_large.shape[1])))
    student_feat = jnp.where(is_large, padded_large, feat_huge)
    swap = [
        ((j * groups + s) * slots_per + k, (s * groups + j) * slots_per + k)
        for j in range(groups)
        for s in range(groups)
        for k in range(slots_per)
    ]
    student_feat = lax.ppermute(student_feat, ("group", "tensor"), swap)
    teacher_normed = layer_norm(teacher_feat, teacher_gain)
    row_large = own_tensor // slots_per < large_groups[0]
    slim = feat_large.shape[1]
    student_rows = student_feat.shape[0]
    normed_large = layer_norm(student_feat[:, :slim], gain_large)
    normed_large = by_near(normed_large.reshape(student_rows, tensors, -1), halves)
    normed_large = jnp.pad(normed_large, ((0, 0), (0, 0), (0, (wide - slim) // near)))
    normed_huge = layer_norm(student_feat, gain_huge)
    normed_huge = by_near(normed_huge.reshape(student_rows, tensors, -1), halves)
    student_normed = jnp.where(row_large, normed_large, normed_huge)

    weights = jnp.concatenate([teacher_proj, proj_large, proj_huge], axis=0)
    half_width = width // 2
    held = jnp.where(own_core == 0, weights[:, :half_width], weights[:, half_width:])
    held = lax.all_to_all(
        jnp.broadcast_to(held[None], (FAR, *held.shape)),
        "tensor",
        split_axis=0,
        concat_axis=0,
        tiled=True,
        axis_index_groups=far_groups,
    )
    lent = lax.ppermute(held, "group", pairs)

    teacher_rows = teacher_feat.shape[0]
    piece = teacher_feat.shape[1] // near
    slot_pad = piece // 2 - wide // near
    teacher_sent = by_near(teacher_normed.reshape(teacher_rows, tensors, -1), halves)
    student_sent = jnp.pad(student_normed, ((0, 0), (0, 0), (0, slot_pad)))
    half = student_rows // 2
    student_sent = jnp.concatenate([student_sent[:, :half], student_sent[:, half:]], axis=2)

    def to_near(values):
        return lax.all_to_all(
            values,
            "tensor",
            split_axis=0,
            concat_axis=0,
            tiled=True,
            axis_index_groups=near_groups,
        )

    row_slot, crop_large = crop_rows(routes, own_group, large_groups[0], slots_per)
    _, other_large = crop_rows(routes, own_group ^ 1, large_groups[0], slots_per)
    near_large = jnp.array(near_groups, dtype=jnp.int32)[own_far] // slots_per < large_groups[0]
    heads = (teacher_proto, center, proto_large, proto_huge)
    live = (row_slot, crop_large, other_large, near_large, own_core, heads)
    cols, live = alone(jnp.concatenate([teacher_sent, student_sent], axis=1), live, to_near)
    cols, held, lent = lax.optimization_barrier((cols, held, lent))
    row_slot, crop_large, other_large, near_large, own_core, heads = live
    held = jnp.concatenate(
        [jnp.where(own_core == 0, held, lent), jnp.where(own_core == 0, lent, held)], axis=2
    )
    first, second = teacher_proj.shape[0], proj_large.shape[0]
    teacher_w = held[:, :first].reshape(-1, width)
    large_w = held[:, first : first + second].reshape(-1, width)
    huge_w = held[:, first + second :].reshape(-1, width)
    teacher_cols = cols[:, :teacher_rows]
    student_cols = jnp.concatenate(
        [
            cols[:, teacher_rows:, : wide // near],
            cols[:, teacher_rows:, piece // 2 : piece // 2 + wide // near],
        ],
        axis=1,
    )
    near_large = near_large[:, None, None]
    zero = jnp.zeros((), jnp.bfloat16)
    part_teacher = jnp.einsum(
        "crf,fb->crb", teacher_cols, teacher_w, preferred_element_type=jnp.float32
    )
    part_student = jnp.einsum(
        "crf,fb->crb",
        jnp.where(near_large, student_cols[:, :, : large_w.shape[0]], zero),
        large_w,
        preferred_element_type=jnp.float32,
    ) + jnp.einsum(
        "crf,fb->crb",
        jnp.where(near_large, zero, student_cols),
        huge_w,
        preferred_element_type=jnp.float32,
    )
    live = (row_slot, crop_large, other_large, own_core, heads)
    parts, live = alone(jnp.concatenate([part_teacher, part_student], axis=1), live, to_near)
    units = jnp.broadcast_to(
        unit_rows(jnp.sum(parts, axis=0))[None], (tensors, parts.shape[1], width)
    )

    def to_all(values):
        return lax.all_to_all(values, "tensor", split_axis=0, concat_axis=0, tiled=True)

    units, live = alone(units, live, to_all)
    row_slot, crop_large, other_large, own_core, heads = live
    teacher_proto, center, proto_large, proto_huge = heads
    chosen = (
        row_slot[:, None] == jnp.arange(tensors * PATCH, dtype=jnp.int32)[None, :]
    ).astype(jnp.bfloat16)
    kept_rows = crop_large == (own_core == 0)
    other_rows = other_large == (own_core == 0)
    teacher_units = units[:, :teacher_rows].reshape(-1, width)
    slot_units = units[:, teacher_rows:].reshape(-1, width)

    student_units = jnp.dot(chosen, slot_units, preferred_element_type=jnp.float32).astype(
        jnp.bfloat16
    )
    both_units = jnp.concatenate(
        [jnp.where(crop_large, student_units, zero), jnp.where(crop_large, zero, student_units)],
        axis=1,
    )
    both_protos = jnp.concatenate([proto_large, proto_huge], axis=0)
    shifted = (
        jnp.dot(teacher_units, teacher_proto, preferred_element_type=jnp.float32) - center[None, :]
    ) / TEACHER_TEMP
    scores = jnp.dot(both_units, both_protos, preferred_element_type=jnp.float32) / STUDENT_TEMP

    teacher_top = jnp.max(shifted, axis=1)
    teacher_exp = jnp.exp(shifted - teacher_top[:, None])
    teacher_sum = jnp.sum(teacher_exp, axis=1)
    student_top = jnp.max(scores, axis=1)
    student_sum = jnp.sum(jnp.exp(scores - student_top[:, None]), axis=1)
    stats = jnp.stack(
        [
            teacher_top + jnp.log(teacher_sum),
            jnp.sum(teacher_exp * scores, axis=1) / teacher_sum,
            student_top + jnp.log(student_sum),
        ]
    )
    stats = jnp.broadcast_to(stats.reshape(1, -1, 128), (tensors, stats.size // 128, 128))
    live = (shifted, scores, student_units, kept_rows, other_rows, own_core)
    stats, live = alone(stats, live, to_all)
    shifted, scores, student_units, kept_rows, other_rows, own_core = live
    stats = stats.reshape(tensors, 3, -1)
    log_t = log_total(stats[:, 0])
    crossed = jnp.sum(stats[:, 1] * jnp.exp(stats[:, 0] - log_t[None, :]), axis=0)
    log_s = log_total(stats[:, 2])
    group_loss = jnp.sum((log_s - crossed).reshape(-1, 128), axis=0)
    target = lax.reduce_precision(jnp.exp(shifted - log_t[:, None]), 8, 7)
    student_prob = jnp.exp(scores - log_s[:, None])
    deltas = ((student_prob - target) / STUDENT_TEMP).astype(jnp.bfloat16)

    rows = deltas.shape[0]
    note = jnp.pad(parts_of(group_loss), ((0, PATCH - 3), (0, protos + width - 128)))
    got = lax.ppermute(
        jnp.concatenate([jnp.concatenate([deltas, student_units], axis=1), note], axis=0),
        "group",
        pairs,
    )
    chip_grad = partial_grad(jnp.where(kept_rows, student_units, zero), deltas) + partial_grad(
        jnp.where(other_rows, got[:rows, protos:], zero), got[:rows, :protos]
    )
    chip_loss = group_loss + jnp.sum(got[rows : rows + 3, :128].astype(jnp.float32), axis=0)
    chips = groups // 2
    grad_rows = width // chips
    note = jnp.pad(parts_of(chip_loss), ((0, grad_rows - 3), (0, 0)))
    sent = jnp.concatenate(
        [
            chip_grad.astype(jnp.bfloat16).reshape(chips, grad_rows, protos),
            jnp.broadcast_to(note[None], (chips, grad_rows, 128)),
        ],
        axis=2,
    )
    same_core = [[core + 2 * chip for chip in range(chips)] for core in range(2)]
    taken = lax.all_to_all(
        sent, "group", split_axis=0, concat_axis=0, tiled=True, axis_index_groups=same_core
    )
    loss = (
        jnp.sum(taken[:, :3, protos:].astype(jnp.float32)) / (routes.shape[0] * PATCH)
    ).reshape(1)
    summed = jnp.sum(taken[:, :, :protos].astype(jnp.float32), axis=0) / PATCH
    mine = lax.all_to_all(
        jnp.broadcast_to(summed.astype(jnp.bfloat16)[None], (chips, grad_rows, protos)),
        "group",
        split_axis=0,
        concat_axis=0,
        tiled=True,
        axis_index_groups=same_core,
    ).reshape(width, protos)
    other = lax.ppermute(mine, "group", pairs)
    return (
        loss,
        jnp.where(own_core == 0, mine, other),
        jnp.where(own_core == 0, other, mine),
    )


def solution(mesh):
    placed = (
        P(("group", "tensor"), None),
        P(),
        P("tensor", None),
        P(None, "tensor"),
        P("tensor"),
        P(),
        P(),
        P(("group", "tensor"), None),
        P(("group", "tensor"), None),
        P(),
        P(),
        P("tensor", None),
        P("tensor", None),
        P(None, "tensor"),
        P(None, "tensor"),
    )
    return jax.shard_map(
        shards,
        mesh=mesh,
        in_specs=placed,
        out_specs=(P(), P(None, "tensor"), P(None, "tensor")),
        check_vma=False,
    )
```

```python
import jax
import jax.numpy as jnp
from jax import lax
from jax.experimental import pallas as pl
from jax.experimental.pallas import tpu as pltpu
from jax.sharding import PartitionSpec as P

PATCH = 16
CG = 16
FAR = 4


TEACHER_TEMP = 0.07
STUDENT_TEMP = 0.1
EPSILON = 1e-06


def layer_norm(values, gains):
    widened = values.astype(jnp.float32)
    row_mean = jnp.mean(widened, axis=-1, keepdims=True)
    centred = widened - row_mean
    spread = jnp.mean(centred * centred, axis=-1, keepdims=True)
    return (centred * lax.rsqrt(spread + EPSILON) * gains).astype(jnp.bfloat16)


def unit_rows(middle):
    return (middle * lax.rsqrt(jnp.mean(middle * middle, axis=-1, keepdims=True) + EPSILON)).astype(
        jnp.bfloat16
    )


def gather_copies(values, axis):
    copies = jnp.broadcast_to(values[None], (lax.axis_size(axis), *values.shape))
    return lax.all_to_all(copies, axis, split_axis=0, concat_axis=0, tiled=True)


def log_total(logs):
    top = jnp.max(logs, axis=0)
    return top + jnp.log(jnp.sum(jnp.exp(logs - top[None, :]), axis=0))


def by_near(columns, halves):
    rows, tensors, wide = columns.shape
    columns = columns.reshape(rows, halves, FAR, FAR, wide).transpose(1, 3, 0, 2, 4)
    return columns.reshape(tensors // FAR, rows, FAR * wide)


def parts_of(values):
    high = lax.reduce_precision(values, 8, 7)
    middle = lax.reduce_precision(values - high, 8, 7)
    low = lax.reduce_precision(values - high - middle, 8, 7)
    return jnp.stack([high, middle, low]).astype(jnp.bfloat16)


def crop_rows(routes, group, large, places):
    target_group = lax.dynamic_index_in_dim(routes[:, 0].reshape(-1, CG), group, 0, keepdims=False)
    earlier = jnp.arange(CG)[:, None] > jnp.arange(CG)[None, :]
    matching = target_group[:, None] == target_group[None, :]
    slot_rank = jnp.sum((matching & earlier).astype(jnp.int32), axis=1)
    slots = places.shape[1]
    own_places = lax.dynamic_index_in_dim(places, group, 0, keepdims=False)
    crop_slot = target_group * (slots // places.shape[0]) + slot_rank
    named = crop_slot[:, None] == jnp.arange(slots, dtype=jnp.int32)[None, :]
    first_row = jnp.sum(jnp.where(named, own_places[None, :], 0), axis=1) * PATCH
    row_slot = (first_row[:, None] + jnp.arange(PATCH, dtype=jnp.int32)[None, :]).reshape(-1)
    return (row_slot, jnp.repeat(target_group < large, PATCH)[:, None])


def partial_grad(units, deltas):
    return lax.dot_general(
        units, deltas, (((0,), (0,)), ((), ())), preferred_element_type=jnp.float32
    )


def alone(values, live, exchange):
    values, live = lax.optimization_barrier((values, live))
    return lax.optimization_barrier((exchange(values), live))


def around(first, second, count):
    return min((first - second) % count, (second - first) % count)


def hops(first_group, first_tensor, second_group, second_tensor):
    first_x = first_group // 8 * 2 + first_tensor // 16
    second_x = second_group // 8 * 2 + second_tensor // 16
    return (
        around(first_x, second_x, 4)
        + around(first_group // 2, second_group // 2, 4)
        + around(first_tensor, second_tensor, 16)
    )


def best_places(costs):
    count = len(costs)
    rows, cols, match = [0] * (count + 1), [0] * (count + 1), [0] * (count + 1)
    for row in range(1, count + 1):
        match[0], col = row, 0
        least, back, used = [1 << 60] * (count + 1), [0] * (count + 1), [False] * (count + 1)
        while match[col]:
            used[col] = True
            current, step, following = match[col], 1 << 60, 0
            for other in range(1, count + 1):
                if not used[other]:
                    left = costs[current - 1][other - 1] - rows[current] - cols[other]
                    if left < least[other]:
                        least[other], back[other] = left, col
                    if least[other] < step:
                        step, following = least[other], other
            for other in range(count + 1):
                if used[other]:
                    rows[match[other]] += step
                    cols[other] -= step
                else:
                    least[other] -= step
            col = following
        while col:
            match[col] = match[back[col]]
            col = back[col]
    places = [0] * count
    for col in range(1, count + 1):
        places[match[col] - 1] = col - 1
    return places


def slot_places(groups, tensors):
    slots_per = tensors // groups
    return [
        best_places(
            [
                [hops(slot // slots_per, s * slots_per + slot % slots_per, s, t) ** 6 for t in range(tensors)]
                for slot in range(tensors)
            ]
        )
        for s in range(groups)
    ]


def prepare_kernel(flags, teacher_w, large_w, huge_w, large_x, huge_x, weights, student):
    half = weights.shape[2]
    first, second, third = teacher_w.shape[0], large_w.shape[0], huge_w.shape[0]
    low_core = flags[0] == 0
    spare = weights.shape[1] - first - second - third
    end = jnp.concatenate([huge_w[...], jnp.zeros((spare, 2 * half), huge_w.dtype)], axis=0)
    for start, rows in ((0, teacher_w[...]), (first, large_w[...]), (first + second, end)):
        kept = jnp.where(low_core, rows[:, :half], rows[:, half:])
        for place in range(FAR):
            weights[place, start : start + rows.shape[0], :] = kept
    slim = large_x.shape[1]
    is_large = flags[1] != 0
    student[:, :slim] = jnp.where(is_large, large_x[...], huge_x[:, :slim])
    student[:, slim:] = jnp.where(is_large, jnp.zeros_like(huge_x[:, slim:]), huge_x[:, slim:])


def prepare(own_core, is_large, teacher_w, large_w, huge_w, large_x, huge_x):
    rows = teacher_w.shape[0] + large_w.shape[0] + huge_w.shape[0]
    rows += -rows % 16
    flags = jnp.stack([own_core.astype(jnp.int32), is_large.astype(jnp.int32)])
    whole = pl.BlockSpec(memory_space=pltpu.VMEM)
    return pl.pallas_call(
        prepare_kernel,
        out_shape=(
            jax.ShapeDtypeStruct((FAR, rows, teacher_w.shape[1] // 2), jnp.bfloat16),
            jax.ShapeDtypeStruct(huge_x.shape, jnp.bfloat16),
        ),
        in_specs=[pl.BlockSpec(memory_space=pltpu.SMEM)] + [whole] * 5,
        out_specs=(whole, whole),
    )(flags, teacher_w, large_w, huge_w, large_x, huge_x)


def shards(
    teacher_feat,
    teacher_gain,
    teacher_proj,
    teacher_proto,
    center,
    routes,
    large_groups,
    feat_large,
    feat_huge,
    gain_large,
    gain_huge,
    proj_large,
    proj_huge,
    proto_large,
    proto_huge,
):
    groups = lax.axis_size("group")
    tensors = lax.axis_size("tensor")
    own_group = lax.axis_index("group")
    own_tensor = lax.axis_index("tensor")
    protos = teacher_proto.shape[1]
    width = teacher_proto.shape[0]
    slots_per = tensors // groups
    near = tensors // FAR
    halves = tensors // (FAR * FAR)
    own_far = own_tensor // FAR % FAR
    own_core = own_group % 2
    near_groups = [
        [half * FAR * FAR + place * FAR + low for half in range(halves) for low in range(FAR)]
        for place in range(FAR)
    ]
    far_groups = [
        [half * FAR * FAR + place * FAR + low for place in range(FAR)]
        for half in range(halves)
        for low in range(FAR)
    ]
    pairs = [(g, g ^ 1) for g in range(groups)]

    is_large = own_group < large_groups[0]
    wide = feat_huge.shape[1]
    weights, student_feat = prepare(
        own_core, is_large, teacher_proj, proj_large, proj_huge, feat_large, feat_huge
    )
    places = slot_places(groups, tensors)
    owners = [[row.index(place) for place in range(tensors)] for row in places]
    swap = [
        (j * tensors + s * slots_per + k, s * tensors + places[s][j * slots_per + k])
        for j in range(groups)
        for s in range(groups)
        for k in range(slots_per)
    ]
    student_feat = lax.ppermute(student_feat, ("group", "tensor"), swap)
    teacher_normed = layer_norm(teacher_feat, teacher_gain)
    places, owners = jnp.array(places, jnp.int32), jnp.array(owners, jnp.int32)
    own_owners = lax.dynamic_index_in_dim(owners, own_group, 0, keepdims=False)
    large_places = own_owners // slots_per < large_groups[0]
    row_large = lax.dynamic_index_in_dim(large_places, own_tensor, 0, keepdims=False)
    slim = feat_large.shape[1]
    student_rows = student_feat.shape[0]
    normed_large = layer_norm(student_feat[:, :slim], gain_large)
    normed_large = by_near(normed_large.reshape(student_rows, tensors, -1), halves)
    normed_large = jnp.pad(normed_large, ((0, 0), (0, 0), (0, (wide - slim) // near)))
    normed_huge = layer_norm(student_feat, gain_huge)
    normed_huge = by_near(normed_huge.reshape(student_rows, tensors, -1), halves)
    student_normed = jnp.where(row_large, normed_large, normed_huge)

    held = lax.all_to_all(
        weights,
        "tensor",
        split_axis=0,
        concat_axis=0,
        tiled=True,
        axis_index_groups=far_groups,
    )
    lent = lax.ppermute(held, "group", pairs)

    teacher_rows = teacher_feat.shape[0]
    piece = teacher_feat.shape[1] // near
    slot_pad = piece // 2 - wide // near
    teacher_sent = by_near(teacher_normed.reshape(teacher_rows, tensors, -1), halves)
    student_sent = jnp.pad(student_normed, ((0, 0), (0, 0), (0, slot_pad)))
    half = student_rows // 2
    student_sent = jnp.concatenate([student_sent[:, :half], student_sent[:, half:]], axis=2)

    def to_near(values):
        return lax.all_to_all(
            values,
            "tensor",
            split_axis=0,
            concat_axis=0,
            tiled=True,
            axis_index_groups=near_groups,
        )

    row_slot, crop_large = crop_rows(routes, own_group, large_groups[0], places)
    _, other_large = crop_rows(routes, own_group ^ 1, large_groups[0], places)
    near_large = lax.dynamic_index_in_dim(
        large_places.reshape(halves, FAR, FAR), own_far, 1, keepdims=False
    ).reshape(-1)
    heads = (teacher_proto, center, proto_large, proto_huge)
    live = (row_slot, crop_large, other_large, near_large, own_core, heads)
    cols, live = alone(jnp.concatenate([teacher_sent, student_sent], axis=1), live, to_near)
    cols, held, lent = lax.optimization_barrier((cols, held, lent))
    row_slot, crop_large, other_large, near_large, own_core, heads = live
    held = jnp.concatenate(
        [jnp.where(own_core == 0, held, lent), jnp.where(own_core == 0, lent, held)], axis=2
    )
    first, second = teacher_proj.shape[0], proj_large.shape[0]
    teacher_w = held[:, :first].reshape(-1, width)
    large_w = held[:, first : first + second].reshape(-1, width)
    huge_w = held[:, first + second : first + second + proj_huge.shape[0]].reshape(-1, width)
    teacher_cols = cols[:, :teacher_rows]
    student_cols = jnp.concatenate(
        [
            cols[:, teacher_rows:, : wide // near],
            cols[:, teacher_rows:, piece // 2 : piece // 2 + wide // near],
        ],
        axis=1,
    )
    near_large = near_large[:, None, None]
    zero = jnp.zeros((), jnp.bfloat16)
    part_teacher = jnp.einsum(
        "crf,fb->crb", teacher_cols, teacher_w, preferred_element_type=jnp.float32
    )
    part_student = jnp.einsum(
        "crf,fb->crb",
        jnp.where(near_large, student_cols[:, :, : large_w.shape[0]], zero),
        large_w,
        preferred_element_type=jnp.float32,
    ) + jnp.einsum(
        "crf,fb->crb",
        jnp.where(near_large, zero, student_cols),
        huge_w,
        preferred_element_type=jnp.float32,
    )
    live = (row_slot, crop_large, other_large, own_core, heads)
    parts, live = alone(jnp.concatenate([part_teacher, part_student], axis=1), live, to_near)
    units = unit_rows(jnp.sum(parts, axis=0))
    ring = tensors // halves
    rings = [[half * ring + place for place in range(ring)] for half in range(halves)]
    across = [[place, place + ring] for place in range(ring)]

    def to_ring(values):
        return lax.all_to_all(
            values, "tensor", split_axis=0, concat_axis=0, tiled=True, axis_index_groups=rings
        )

    def to_tensor(values):
        return lax.all_to_all(values, "tensor", split_axis=0, concat_axis=0, tiled=True)

    def to_half(values):
        return lax.all_gather(values, "tensor", axis=0, tiled=True, axis_index_groups=across)

    units, live = alone(jnp.broadcast_to(units[None], (ring, *units.shape)), live, to_ring)
    units, live = alone(units, live, to_half)
    row_slot, crop_large, other_large, own_core, heads = live
    teacher_proto, center, proto_large, proto_huge = heads
    chosen = (
        row_slot[:, None] == jnp.arange(tensors * PATCH, dtype=jnp.int32)[None, :]
    ).astype(jnp.bfloat16)
    kept_rows = crop_large == (own_core == 0)
    other_rows = other_large == (own_core == 0)
    teacher_units = units[:, :teacher_rows].reshape(-1, width)
    slot_units = units[:, teacher_rows:].reshape(-1, width)

    student_units = jnp.dot(chosen, slot_units, preferred_element_type=jnp.float32).astype(
        jnp.bfloat16
    )
    both_units = jnp.concatenate(
        [jnp.where(crop_large, student_units, zero), jnp.where(crop_large, zero, student_units)],
        axis=1,
    )
    both_protos = jnp.concatenate([proto_large, proto_huge], axis=0)
    shifted = (
        jnp.dot(teacher_units, teacher_proto, preferred_element_type=jnp.float32) - center[None, :]
    ) / TEACHER_TEMP
    scores = jnp.dot(both_units, both_protos, preferred_element_type=jnp.float32) / STUDENT_TEMP

    teacher_top = jnp.max(shifted, axis=1)
    teacher_exp = jnp.exp(shifted - teacher_top[:, None])
    teacher_sum = jnp.sum(teacher_exp, axis=1)
    student_top = jnp.max(scores, axis=1)
    student_sum = jnp.sum(jnp.exp(scores - student_top[:, None]), axis=1)
    stats = jnp.stack(
        [
            teacher_top + jnp.log(teacher_sum),
            jnp.sum(teacher_exp * scores, axis=1) / teacher_sum,
            student_top + jnp.log(student_sum),
        ]
    )
    stats = jnp.broadcast_to(stats.reshape(1, -1, 128), (tensors, stats.size // 128, 128))
    live = (shifted, scores, student_units, kept_rows, other_rows, own_core)
    stats, live = alone(stats, live, to_tensor)
    shifted, scores, student_units, kept_rows, other_rows, own_core = live
    stats = stats.reshape(tensors, 3, -1)
    log_t = log_total(stats[:, 0])
    crossed = jnp.sum(stats[:, 1] * jnp.exp(stats[:, 0] - log_t[None, :]), axis=0)
    log_s = log_total(stats[:, 2])
    group_loss = jnp.sum((log_s - crossed).reshape(-1, 128), axis=0)
    target = lax.reduce_precision(jnp.exp(shifted - log_t[:, None]), 8, 7)
    student_prob = jnp.exp(scores - log_s[:, None])
    deltas = ((student_prob - target) / STUDENT_TEMP).astype(jnp.bfloat16)

    rows = deltas.shape[0]
    note = jnp.pad(parts_of(group_loss), ((0, PATCH - 3), (0, protos + width - 128)))
    got = lax.ppermute(
        jnp.concatenate([jnp.concatenate([deltas, student_units], axis=1), note], axis=0),
        "group",
        pairs,
    )
    chip_grad = partial_grad(jnp.where(kept_rows, student_units, zero), deltas) + partial_grad(
        jnp.where(other_rows, got[:rows, protos:], zero), got[:rows, :protos]
    )
    chip_loss = group_loss + jnp.sum(got[rows : rows + 3, :128].astype(jnp.float32), axis=0)
    chips = groups // 2
    grad_rows = width // chips
    note = jnp.pad(parts_of(chip_loss), ((0, grad_rows - 3), (0, 0)))
    sent = jnp.concatenate(
        [
            chip_grad.astype(jnp.bfloat16).reshape(chips, grad_rows, protos),
            jnp.broadcast_to(note[None], (chips, grad_rows, 128)),
        ],
        axis=2,
    )
    same_core = [[core + 2 * chip for chip in range(chips)] for core in range(2)]
    taken = lax.all_to_all(
        sent, "group", split_axis=0, concat_axis=0, tiled=True, axis_index_groups=same_core
    )
    loss = (
        jnp.sum(taken[:, :3, protos:].astype(jnp.float32)) / (routes.shape[0] * PATCH)
    ).reshape(1)
    summed = jnp.sum(taken[:, :, :protos].astype(jnp.float32), axis=0) / PATCH
    mine = lax.all_to_all(
        jnp.broadcast_to(summed.astype(jnp.bfloat16)[None], (chips, grad_rows, protos)),
        "group",
        split_axis=0,
        concat_axis=0,
        tiled=True,
        axis_index_groups=same_core,
    ).reshape(width, protos)
    other = lax.ppermute(mine, "group", pairs)
    return (
        loss,
        jnp.where(own_core == 0, mine, other),
        jnp.where(own_core == 0, other, mine),
    )


def solution(mesh):
    placed = (
        P(("group", "tensor"), None),
        P(),
        P("tensor", None),
        P(None, "tensor"),
        P("tensor"),
        P(),
        P(),
        P(("group", "tensor"), None),
        P(("group", "tensor"), None),
        P(),
        P(),
        P("tensor", None),
        P("tensor", None),
        P(None, "tensor"),
        P(None, "tensor"),
    )
    return jax.shard_map(
        shards,
        mesh=mesh,
        in_specs=placed,
        out_specs=(P(), P(None, "tensor"), P(None, "tensor")),
        check_vma=False,
    )
```

```python
import jax
import jax.numpy as jnp
from jax import lax
from jax.experimental import pallas as pl
from jax.experimental.pallas import tpu as pltpu
from jax.sharding import PartitionSpec as P

PATCH = 16
CG = 16
FAR = 4


TEACHER_TEMP = 0.07
STUDENT_TEMP = 0.1
EPSILON = 1e-06


def unit_rows(middle):
    return (middle * lax.rsqrt(jnp.mean(middle * middle, axis=-1, keepdims=True) + EPSILON)).astype(
        jnp.bfloat16
    )


def gather_copies(values, axis):
    copies = jnp.broadcast_to(values[None], (lax.axis_size(axis), *values.shape))
    return lax.all_to_all(copies, axis, split_axis=0, concat_axis=0, tiled=True)


def log_total(logs):
    top = jnp.max(logs, axis=0)
    return top + jnp.log(jnp.sum(jnp.exp(logs - top[None, :]), axis=0))


def parts_of(values):
    high = lax.reduce_precision(values, 8, 7)
    middle = lax.reduce_precision(values - high, 8, 7)
    low = lax.reduce_precision(values - high - middle, 8, 7)
    return jnp.stack([high, middle, low]).astype(jnp.bfloat16)


def crop_rows(routes, group, large, places):
    target_group = lax.dynamic_index_in_dim(routes[:, 0].reshape(-1, CG), group, 0, keepdims=False)
    earlier = jnp.arange(CG)[:, None] > jnp.arange(CG)[None, :]
    matching = target_group[:, None] == target_group[None, :]
    slot_rank = jnp.sum((matching & earlier).astype(jnp.int32), axis=1)
    slots = places.shape[1]
    own_places = lax.dynamic_index_in_dim(places, group, 0, keepdims=False)
    crop_slot = target_group * (slots // places.shape[0]) + slot_rank
    named = crop_slot[:, None] == jnp.arange(slots, dtype=jnp.int32)[None, :]
    first_row = jnp.sum(jnp.where(named, own_places[None, :], 0), axis=1) * PATCH
    row_slot = (first_row[:, None] + jnp.arange(PATCH, dtype=jnp.int32)[None, :]).reshape(-1)
    return (row_slot, jnp.repeat(target_group < large, PATCH)[:, None])


def partial_grad(units, deltas):
    return lax.dot_general(
        units, deltas, (((0,), (0,)), ((), ())), preferred_element_type=jnp.float32
    )


def alone(values, live, exchange):
    values, live = lax.optimization_barrier((values, live))
    return lax.optimization_barrier((exchange(values), live))


def around(first, second, count):
    return min((first - second) % count, (second - first) % count)


def hops(first_group, first_tensor, second_group, second_tensor):
    first_x = first_group // 8 * 2 + first_tensor // 16
    second_x = second_group // 8 * 2 + second_tensor // 16
    return (
        around(first_x, second_x, 4)
        + around(first_group // 2, second_group // 2, 4)
        + around(first_tensor, second_tensor, 16)
    )


def best_places(costs):
    count = len(costs)
    rows, cols, match = [0] * (count + 1), [0] * (count + 1), [0] * (count + 1)
    for row in range(1, count + 1):
        match[0], col = row, 0
        least, back, used = [1 << 60] * (count + 1), [0] * (count + 1), [False] * (count + 1)
        while match[col]:
            used[col] = True
            current, step, following = match[col], 1 << 60, 0
            for other in range(1, count + 1):
                if not used[other]:
                    left = costs[current - 1][other - 1] - rows[current] - cols[other]
                    if left < least[other]:
                        least[other], back[other] = left, col
                    if least[other] < step:
                        step, following = least[other], other
            for other in range(count + 1):
                if used[other]:
                    rows[match[other]] += step
                    cols[other] -= step
                else:
                    least[other] -= step
            col = following
        while col:
            match[col] = match[back[col]]
            col = back[col]
    places = [0] * count
    for col in range(1, count + 1):
        places[match[col] - 1] = col - 1
    return places


def slot_places(groups, tensors):
    slots_per = tensors // groups
    return [
        best_places(
            [
                [hops(slot // slots_per, s * slots_per + slot % slots_per, s, t) ** 6 for t in range(tensors)]
                for slot in range(tensors)
            ]
        )
        for s in range(groups)
    ]


def normed_rows(values, gains):
    row_mean = jnp.mean(values, axis=-1, keepdims=True)
    centred = values - row_mean
    spread = jnp.mean(centred * centred, axis=-1, keepdims=True)
    return centred * lax.rsqrt(spread + EPSILON) * gains


def near_columns(values, tensors, dest):
    wide = values.shape[1] // tensors
    half, low = dest // FAR, dest % FAR
    places = [(half * FAR + place) * FAR + low for place in range(FAR)]
    return [values[:, place * wide : (place + 1) * wide] for place in places]


def prepare_kernel(
    teacher_w, large_w, huge_w, teacher_x, gain, weights, sent
):
    own_group = lax.axis_index("group")
    half = weights.shape[2]
    first, second, third = teacher_w.shape[0], large_w.shape[0], huge_w.shape[0]
    low_core = lax.rem(own_group, 2) == 0
    spare = weights.shape[1] - first - second - third
    end = jnp.concatenate([huge_w[...], jnp.zeros((spare, 2 * half), huge_w.dtype)], axis=0)
    for start, rows in ((0, teacher_w[...]), (first, large_w[...]), (first + second, end)):
        kept = jnp.where(low_core, rows[:, :half], rows[:, half:])
        for place in range(FAR):
            weights[place, start : start + rows.shape[0], :] = kept
    normed = normed_rows(teacher_x[...].astype(jnp.float32), gain[...]).astype(jnp.bfloat16)
    tensors = sent.shape[0] * FAR
    for dest in range(sent.shape[0]):
        sent[dest] = jnp.concatenate(near_columns(normed, tensors, dest), axis=1)


def prepare(teacher_w, large_w, huge_w, teacher_x, gain, near):
    rows = teacher_w.shape[0] + large_w.shape[0] + huge_w.shape[0]
    rows += -rows % 16
    whole = pl.BlockSpec(memory_space=pltpu.VMEM)
    return pl.pallas_call(
        prepare_kernel,
        out_shape=(
            jax.ShapeDtypeStruct((FAR, rows, teacher_w.shape[1] // 2), jnp.bfloat16),
            jax.ShapeDtypeStruct((near, teacher_x.shape[0], teacher_x.shape[1] // near), jnp.bfloat16),
        ),
        in_specs=[whole] * 5,
        out_specs=(whole, whole),
    )(teacher_w, large_w, huge_w, teacher_x, gain.reshape(1, -1))


def student_kernel(large_groups, owners, student, gain_large, gain_huge, teacher, sent):
    own_group, own_tensor = lax.axis_index("group"), lax.axis_index("tensor")
    groups, tensors = owners.shape
    is_large = owners[own_group, own_tensor] // (tensors // groups) < large_groups[0]
    rows = teacher.shape[1]

    def send(normed):
        for dest in range(sent.shape[0]):
            columns = near_columns(normed, tensors, dest)
            filled = FAR * columns[0].shape[1]
            columns.append(jnp.zeros((2 * rows, sent.shape[2] // 2 - filled), jnp.float32))
            block = jnp.concatenate(columns, axis=1)
            block = jnp.concatenate([block[:rows], block[rows:]], axis=1)
            block = jnp.concatenate([teacher[dest].astype(jnp.float32), block], axis=0)
            sent[dest] = block.astype(jnp.bfloat16)

    @pl.when(is_large)
    def _():
        send(normed_rows(student[:, : gain_large.shape[1]].astype(jnp.float32), gain_large[...]))

    @pl.when(jnp.logical_not(is_large))
    def _():
        send(normed_rows(student[...].astype(jnp.float32), gain_huge[...]))


def student_columns(large_groups, owners, student, gain_large, gain_huge, teacher):
    near, rows, wide = teacher.shape
    whole = pl.BlockSpec(memory_space=pltpu.VMEM)
    scalars = pl.BlockSpec(memory_space=pltpu.SMEM)
    return pl.pallas_call(
        student_kernel,
        out_shape=jax.ShapeDtypeStruct((near, 2 * rows, wide), jnp.bfloat16),
        in_specs=[scalars, scalars] + [whole] * 4,
        out_specs=whole,
    )(large_groups, owners, student, gain_large.reshape(1, -1), gain_huge.reshape(1, -1), teacher)


def shards(
    teacher_feat,
    teacher_gain,
    teacher_proj,
    teacher_proto,
    center,
    routes,
    large_groups,
    feat_large,
    feat_huge,
    gain_large,
    gain_huge,
    proj_large,
    proj_huge,
    proto_large,
    proto_huge,
):
    groups = lax.axis_size("group")
    tensors = lax.axis_size("tensor")
    own_group = lax.axis_index("group")
    own_tensor = lax.axis_index("tensor")
    protos = teacher_proto.shape[1]
    width = teacher_proto.shape[0]
    slots_per = tensors // groups
    near = tensors // FAR
    halves = tensors // (FAR * FAR)
    own_far = own_tensor // FAR % FAR
    own_core = own_group % 2
    near_groups = [
        [half * FAR * FAR + place * FAR + low for half in range(halves) for low in range(FAR)]
        for place in range(FAR)
    ]
    far_groups = [
        [half * FAR * FAR + place * FAR + low for place in range(FAR)]
        for half in range(halves)
        for low in range(FAR)
    ]
    pairs = [(g, g ^ 1) for g in range(groups)]

    padded_large = jnp.pad(feat_large, ((0, 0), (0, feat_huge.shape[1] - feat_large.shape[1])))
    student_feat = jnp.where(own_group < large_groups[0], padded_large, feat_huge)
    weights, teacher_sent = prepare(
        teacher_proj, proj_large, proj_huge, teacher_feat, teacher_gain, near
    )
    places = slot_places(groups, tensors)
    owners = [[row.index(place) for place in range(tensors)] for row in places]
    swap = [
        (j * tensors + s * slots_per + k, s * tensors + places[s][j * slots_per + k])
        for j in range(groups)
        for s in range(groups)
        for k in range(slots_per)
    ]
    student_feat = lax.ppermute(student_feat, ("group", "tensor"), swap)
    places, owners = jnp.array(places, jnp.int32), jnp.array(owners, jnp.int32)
    own_owners = lax.dynamic_index_in_dim(owners, own_group, 0, keepdims=False)
    large_places = own_owners // slots_per < large_groups[0]

    held = lax.all_to_all(
        weights,
        "tensor",
        split_axis=0,
        concat_axis=0,
        tiled=True,
        axis_index_groups=far_groups,
    )
    lent = lax.ppermute(held, "group", pairs)

    teacher_rows, wide = teacher_feat.shape[0], feat_huge.shape[1]
    piece = teacher_feat.shape[1] // near
    sent = student_columns(
        large_groups, owners, student_feat, gain_large, gain_huge, teacher_sent
    )

    def to_near(values):
        return lax.all_to_all(
            values,
            "tensor",
            split_axis=0,
            concat_axis=0,
            tiled=True,
            axis_index_groups=near_groups,
        )

    row_slot, crop_large = crop_rows(routes, own_group, large_groups[0], places)
    _, other_large = crop_rows(routes, own_group ^ 1, large_groups[0], places)
    near_large = lax.dynamic_index_in_dim(
        large_places.reshape(halves, FAR, FAR), own_far, 1, keepdims=False
    ).reshape(-1)
    heads = (teacher_proto, center, proto_large, proto_huge)
    live = (row_slot, crop_large, other_large, near_large, own_core, heads)
    cols, live = alone(sent, live, to_near)
    cols, held, lent = lax.optimization_barrier((cols, held, lent))
    row_slot, crop_large, other_large, near_large, own_core, heads = live
    held = jnp.concatenate(
        [jnp.where(own_core == 0, held, lent), jnp.where(own_core == 0, lent, held)], axis=2
    )
    first, second = teacher_proj.shape[0], proj_large.shape[0]
    teacher_w = held[:, :first].reshape(-1, width)
    large_w = held[:, first : first + second].reshape(-1, width)
    huge_w = held[:, first + second : first + second + proj_huge.shape[0]].reshape(-1, width)
    teacher_cols = cols[:, :teacher_rows]
    student_cols = jnp.concatenate(
        [
            cols[:, teacher_rows:, : wide // near],
            cols[:, teacher_rows:, piece // 2 : piece // 2 + wide // near],
        ],
        axis=1,
    )
    near_large = near_large[:, None, None]
    zero = jnp.zeros((), jnp.bfloat16)
    part_teacher = jnp.einsum(
        "crf,fb->crb", teacher_cols, teacher_w, preferred_element_type=jnp.float32
    )
    part_student = jnp.einsum(
        "crf,fb->crb",
        jnp.where(near_large, student_cols[:, :, : large_w.shape[0]], zero),
        large_w,
        preferred_element_type=jnp.float32,
    ) + jnp.einsum(
        "crf,fb->crb",
        jnp.where(near_large, zero, student_cols),
        huge_w,
        preferred_element_type=jnp.float32,
    )
    live = (row_slot, crop_large, other_large, own_core, heads)
    parts, live = alone(jnp.concatenate([part_teacher, part_student], axis=1), live, to_near)
    units = unit_rows(jnp.sum(parts, axis=0))
    ring = tensors // halves
    rings = [[half * ring + place for place in range(ring)] for half in range(halves)]
    across = [[place, place + ring] for place in range(ring)]

    def to_ring(values):
        return lax.all_to_all(
            values, "tensor", split_axis=0, concat_axis=0, tiled=True, axis_index_groups=rings
        )

    def to_tensor(values):
        return lax.all_to_all(values, "tensor", split_axis=0, concat_axis=0, tiled=True)

    def to_half(values):
        return lax.all_gather(values, "tensor", axis=0, tiled=True, axis_index_groups=across)

    units, live = alone(jnp.broadcast_to(units[None], (ring, *units.shape)), live, to_ring)
    units, live = alone(units, live, to_half)
    row_slot, crop_large, other_large, own_core, heads = live
    teacher_proto, center, proto_large, proto_huge = heads
    chosen = (
        row_slot[:, None] == jnp.arange(tensors * PATCH, dtype=jnp.int32)[None, :]
    ).astype(jnp.bfloat16)
    kept_rows = crop_large == (own_core == 0)
    other_rows = other_large == (own_core == 0)
    teacher_units = units[:, :teacher_rows].reshape(-1, width)
    slot_units = units[:, teacher_rows:].reshape(-1, width)

    student_units = jnp.dot(chosen, slot_units, preferred_element_type=jnp.float32).astype(
        jnp.bfloat16
    )
    both_units = jnp.concatenate(
        [jnp.where(crop_large, student_units, zero), jnp.where(crop_large, zero, student_units)],
        axis=1,
    )
    both_protos = jnp.concatenate([proto_large, proto_huge], axis=0)
    shifted = (
        jnp.dot(teacher_units, teacher_proto, preferred_element_type=jnp.float32) - center[None, :]
    ) / TEACHER_TEMP
    scores = jnp.dot(both_units, both_protos, preferred_element_type=jnp.float32) / STUDENT_TEMP

    teacher_top = jnp.max(shifted, axis=1)
    teacher_exp = jnp.exp(shifted - teacher_top[:, None])
    teacher_sum = jnp.sum(teacher_exp, axis=1)
    student_top = jnp.max(scores, axis=1)
    student_sum = jnp.sum(jnp.exp(scores - student_top[:, None]), axis=1)
    stats = jnp.stack(
        [
            teacher_top + jnp.log(teacher_sum),
            jnp.sum(teacher_exp * scores, axis=1) / teacher_sum,
            student_top + jnp.log(student_sum),
        ]
    )
    stats = jnp.broadcast_to(stats.reshape(1, -1, 128), (tensors, stats.size // 128, 128))
    live = (shifted, scores, student_units, kept_rows, other_rows, own_core)
    stats, live = alone(stats, live, to_tensor)
    shifted, scores, student_units, kept_rows, other_rows, own_core = live
    stats = stats.reshape(tensors, 3, -1)
    log_t = log_total(stats[:, 0])
    crossed = jnp.sum(stats[:, 1] * jnp.exp(stats[:, 0] - log_t[None, :]), axis=0)
    log_s = log_total(stats[:, 2])
    group_loss = jnp.sum((log_s - crossed).reshape(-1, 128), axis=0)
    target = lax.reduce_precision(jnp.exp(shifted - log_t[:, None]), 8, 7)
    student_prob = jnp.exp(scores - log_s[:, None])
    deltas = ((student_prob - target) / STUDENT_TEMP).astype(jnp.bfloat16)

    rows = deltas.shape[0]
    note = jnp.pad(parts_of(group_loss), ((0, PATCH - 3), (0, protos + width - 128)))
    got = lax.ppermute(
        jnp.concatenate([jnp.concatenate([deltas, student_units], axis=1), note], axis=0),
        "group",
        pairs,
    )
    chip_grad = partial_grad(jnp.where(kept_rows, student_units, zero), deltas) + partial_grad(
        jnp.where(other_rows, got[:rows, protos:], zero), got[:rows, :protos]
    )
    chip_loss = group_loss + jnp.sum(got[rows : rows + 3, :128].astype(jnp.float32), axis=0)
    chips = groups // 2
    grad_rows = width // chips
    note = jnp.pad(parts_of(chip_loss), ((0, grad_rows - 3), (0, 0)))
    sent = jnp.concatenate(
        [
            chip_grad.astype(jnp.bfloat16).reshape(chips, grad_rows, protos),
            jnp.broadcast_to(note[None], (chips, grad_rows, 128)),
        ],
        axis=2,
    )
    same_core = [[core + 2 * chip for chip in range(chips)] for core in range(2)]
    taken = lax.all_to_all(
        sent, "group", split_axis=0, concat_axis=0, tiled=True, axis_index_groups=same_core
    )
    loss = (
        jnp.sum(taken[:, :3, protos:].astype(jnp.float32)) / (routes.shape[0] * PATCH)
    ).reshape(1)
    summed = jnp.sum(taken[:, :, :protos].astype(jnp.float32), axis=0) / PATCH
    mine = lax.all_to_all(
        jnp.broadcast_to(summed.astype(jnp.bfloat16)[None], (chips, grad_rows, protos)),
        "group",
        split_axis=0,
        concat_axis=0,
        tiled=True,
        axis_index_groups=same_core,
    ).reshape(width, protos)
    other = lax.ppermute(mine, "group", pairs)
    return (
        loss,
        jnp.where(own_core == 0, mine, other),
        jnp.where(own_core == 0, other, mine),
    )


def solution(mesh):
    placed = (
        P(("group", "tensor"), None),
        P(),
        P("tensor", None),
        P(None, "tensor"),
        P("tensor"),
        P(),
        P(),
        P(("group", "tensor"), None),
        P(("group", "tensor"), None),
        P(),
        P(),
        P("tensor", None),
        P("tensor", None),
        P(None, "tensor"),
        P(None, "tensor"),
    )
    return jax.shard_map(
        shards,
        mesh=mesh,
        in_specs=placed,
        out_specs=(P(), P(None, "tensor"), P(None, "tensor")),
        check_vma=False,
    )
```

```python
import jax
import jax.numpy as jnp
from jax import lax
from jax.experimental import pallas as pl
from jax.experimental.pallas import tpu as pltpu
from jax.sharding import PartitionSpec as P

PATCH = 16
CG = 16
FAR = 4


TEACHER_TEMP = 0.07
STUDENT_TEMP = 0.1
EPSILON = 1e-06


def unit_rows(middle):
    return (middle * lax.rsqrt(jnp.mean(middle * middle, axis=-1, keepdims=True) + EPSILON)).astype(
        jnp.bfloat16
    )


def gather_copies(values, axis):
    copies = jnp.broadcast_to(values[None], (lax.axis_size(axis), *values.shape))
    return lax.all_to_all(copies, axis, split_axis=0, concat_axis=0, tiled=True)


def log_total(logs):
    top = jnp.max(logs, axis=0)
    return top + jnp.log(jnp.sum(jnp.exp(logs - top[None, :]), axis=0))


def parts_of(values):
    high = lax.reduce_precision(values, 8, 7)
    middle = lax.reduce_precision(values - high, 8, 7)
    low = lax.reduce_precision(values - high - middle, 8, 7)
    return jnp.stack([high, middle, low]).astype(jnp.bfloat16)


def crop_rows(routes, group, large, places):
    target_group = lax.dynamic_index_in_dim(routes[:, 0].reshape(-1, CG), group, 0, keepdims=False)
    earlier = jnp.arange(CG)[:, None] > jnp.arange(CG)[None, :]
    matching = target_group[:, None] == target_group[None, :]
    slot_rank = jnp.sum((matching & earlier).astype(jnp.int32), axis=1)
    slots = places.shape[1]
    own_places = lax.dynamic_index_in_dim(places, group, 0, keepdims=False)
    crop_slot = target_group * (slots // places.shape[0]) + slot_rank
    named = crop_slot[:, None] == jnp.arange(slots, dtype=jnp.int32)[None, :]
    first_row = jnp.sum(jnp.where(named, own_places[None, :], 0), axis=1) * PATCH
    row_slot = (first_row[:, None] + jnp.arange(PATCH, dtype=jnp.int32)[None, :]).reshape(-1)
    return (row_slot, jnp.repeat(target_group < large, PATCH)[:, None])


def partial_grad(units, deltas):
    return lax.dot_general(
        units, deltas, (((0,), (0,)), ((), ())), preferred_element_type=jnp.float32
    )


def alone(values, live, exchange):
    values, live = lax.optimization_barrier((values, live))
    return lax.optimization_barrier((exchange(values), live))


def around(first, second, count):
    return min((first - second) % count, (second - first) % count)


def hops(first_group, first_tensor, second_group, second_tensor):
    first_x = first_group // 8 * 2 + first_tensor // 16
    second_x = second_group // 8 * 2 + second_tensor // 16
    return (
        around(first_x, second_x, 4)
        + around(first_group // 2, second_group // 2, 4)
        + around(first_tensor, second_tensor, 16)
    )


def best_places(costs):
    count = len(costs)
    rows, cols, match = [0] * (count + 1), [0] * (count + 1), [0] * (count + 1)
    for row in range(1, count + 1):
        match[0], col = row, 0
        least, back, used = [1 << 60] * (count + 1), [0] * (count + 1), [False] * (count + 1)
        while match[col]:
            used[col] = True
            current, step, following = match[col], 1 << 60, 0
            for other in range(1, count + 1):
                if not used[other]:
                    left = costs[current - 1][other - 1] - rows[current] - cols[other]
                    if left < least[other]:
                        least[other], back[other] = left, col
                    if least[other] < step:
                        step, following = least[other], other
            for other in range(count + 1):
                if used[other]:
                    rows[match[other]] += step
                    cols[other] -= step
                else:
                    least[other] -= step
            col = following
        while col:
            match[col] = match[back[col]]
            col = back[col]
    places = [0] * count
    for col in range(1, count + 1):
        places[match[col] - 1] = col - 1
    return places


def slot_places(groups, tensors):
    slots_per = tensors // groups
    return [
        best_places(
            [
                [hops(slot // slots_per, s * slots_per + slot % slots_per, s, t) ** 6 for t in range(tensors)]
                for slot in range(tensors)
            ]
        )
        for s in range(groups)
    ]


def normed_rows(values, gains):
    row_mean = jnp.mean(values, axis=-1, keepdims=True)
    centred = values - row_mean
    spread = jnp.mean(centred * centred, axis=-1, keepdims=True)
    return centred * lax.rsqrt(spread + EPSILON) * gains


def near_columns(values, tensors, dest):
    wide = values.shape[1] // tensors
    half, low = dest // FAR, dest % FAR
    places = [(half * FAR + place) * FAR + low for place in range(FAR)]
    return [values[:, place * wide : (place + 1) * wide] for place in places]


def prepare_kernel(
    teacher_w, large_w, huge_w, teacher_x, gain, weights, sent
):
    own_group = lax.axis_index("group")
    half = weights.shape[2]
    first, second, third = teacher_w.shape[0], large_w.shape[0], huge_w.shape[0]
    low_core = lax.rem(own_group, 2) == 0
    spare = weights.shape[1] - first - second - third
    end = jnp.concatenate([huge_w[...], jnp.zeros((spare, 2 * half), huge_w.dtype)], axis=0)
    for start, rows in ((0, teacher_w[...]), (first, large_w[...]), (first + second, end)):
        kept = jnp.where(low_core, rows[:, :half], rows[:, half:])
        for place in range(FAR):
            weights[place, start : start + rows.shape[0], :] = kept
    normed = normed_rows(teacher_x[...].astype(jnp.float32), gain[...])
    tensors = sent.shape[0] * FAR
    for dest in range(sent.shape[0]):
        sent[dest] = jnp.concatenate(near_columns(normed, tensors, dest), axis=1)


def prepare(teacher_w, large_w, huge_w, teacher_x, gain, near):
    rows = teacher_w.shape[0] + large_w.shape[0] + huge_w.shape[0]
    rows += -rows % 16
    whole = pl.BlockSpec(memory_space=pltpu.VMEM)
    return pl.pallas_call(
        prepare_kernel,
        out_shape=(
            jax.ShapeDtypeStruct((FAR, rows, teacher_w.shape[1] // 2), jnp.bfloat16),
            jax.ShapeDtypeStruct((near, teacher_x.shape[0], teacher_x.shape[1] // near), jnp.float32),
        ),
        in_specs=[whole] * 5,
        out_specs=(whole, whole),
    )(teacher_w, large_w, huge_w, teacher_x, gain.reshape(1, -1))


def student_kernel(large_groups, owners, student, gain_large, gain_huge, teacher, sent):
    own_group, own_tensor = lax.axis_index("group"), lax.axis_index("tensor")
    groups, tensors = owners.shape
    is_large = owners[own_group, own_tensor] // (tensors // groups) < large_groups[0]
    rows = teacher.shape[1]

    def send(normed):
        for dest in range(sent.shape[0]):
            columns = near_columns(normed, tensors, dest)
            filled = FAR * columns[0].shape[1]
            columns.append(jnp.zeros((2 * rows, sent.shape[2] // 2 - filled), jnp.float32))
            block = jnp.concatenate(columns, axis=1)
            block = jnp.concatenate([block[:rows], block[rows:]], axis=1)
            block = jnp.concatenate([teacher[dest], block], axis=0)
            sent[dest] = block.astype(jnp.bfloat16)

    @pl.when(is_large)
    def _():
        send(normed_rows(student[:, : gain_large.shape[1]].astype(jnp.float32), gain_large[...]))

    @pl.when(jnp.logical_not(is_large))
    def _():
        send(normed_rows(student[...].astype(jnp.float32), gain_huge[...]))


def student_columns(large_groups, owners, student, gain_large, gain_huge, teacher):
    near, rows, wide = teacher.shape
    whole = pl.BlockSpec(memory_space=pltpu.VMEM)
    scalars = pl.BlockSpec(memory_space=pltpu.SMEM)
    return pl.pallas_call(
        student_kernel,
        out_shape=jax.ShapeDtypeStruct((near, 2 * rows, wide), jnp.bfloat16),
        in_specs=[scalars, scalars] + [whole] * 4,
        out_specs=whole,
    )(large_groups, owners, student, gain_large.reshape(1, -1), gain_huge.reshape(1, -1), teacher)


def shards(
    teacher_feat,
    teacher_gain,
    teacher_proj,
    teacher_proto,
    center,
    routes,
    large_groups,
    feat_large,
    feat_huge,
    gain_large,
    gain_huge,
    proj_large,
    proj_huge,
    proto_large,
    proto_huge,
):
    groups = lax.axis_size("group")
    tensors = lax.axis_size("tensor")
    own_group = lax.axis_index("group")
    own_tensor = lax.axis_index("tensor")
    protos = teacher_proto.shape[1]
    width = teacher_proto.shape[0]
    slots_per = tensors // groups
    near = tensors // FAR
    halves = tensors // (FAR * FAR)
    own_far = own_tensor // FAR % FAR
    own_core = own_group % 2
    near_groups = [
        [half * FAR * FAR + place * FAR + low for half in range(halves) for low in range(FAR)]
        for place in range(FAR)
    ]
    far_groups = [
        [half * FAR * FAR + place * FAR + low for place in range(FAR)]
        for half in range(halves)
        for low in range(FAR)
    ]
    pairs = [(g, g ^ 1) for g in range(groups)]

    padded_large = jnp.pad(feat_large, ((0, 0), (0, feat_huge.shape[1] - feat_large.shape[1])))
    student_feat = jnp.where(own_group < large_groups[0], padded_large, feat_huge)
    weights, teacher_sent = prepare(
        teacher_proj, proj_large, proj_huge, teacher_feat, teacher_gain, near
    )
    places = slot_places(groups, tensors)
    owners = [[row.index(place) for place in range(tensors)] for row in places]
    swap = [
        (j * tensors + s * slots_per + k, s * tensors + places[s][j * slots_per + k])
        for j in range(groups)
        for s in range(groups)
        for k in range(slots_per)
    ]
    student_feat = lax.ppermute(student_feat, ("group", "tensor"), swap)
    places, owners = jnp.array(places, jnp.int32), jnp.array(owners, jnp.int32)
    own_owners = lax.dynamic_index_in_dim(owners, own_group, 0, keepdims=False)
    large_places = own_owners // slots_per < large_groups[0]

    held = lax.all_to_all(
        weights,
        "tensor",
        split_axis=0,
        concat_axis=0,
        tiled=True,
        axis_index_groups=far_groups,
    )
    lent = lax.ppermute(held, "group", pairs)

    teacher_rows, wide = teacher_feat.shape[0], feat_huge.shape[1]
    piece = teacher_feat.shape[1] // near
    sent = student_columns(
        large_groups, owners, student_feat, gain_large, gain_huge, teacher_sent
    )

    def to_near(values):
        return lax.all_to_all(
            values,
            "tensor",
            split_axis=0,
            concat_axis=0,
            tiled=True,
            axis_index_groups=near_groups,
        )

    row_slot, crop_large = crop_rows(routes, own_group, large_groups[0], places)
    _, other_large = crop_rows(routes, own_group ^ 1, large_groups[0], places)
    near_large = lax.dynamic_index_in_dim(
        large_places.reshape(halves, FAR, FAR), own_far, 1, keepdims=False
    ).reshape(-1)
    heads = (teacher_proto, center, proto_large, proto_huge)
    live = (row_slot, crop_large, other_large, near_large, own_core, heads)
    cols, live = alone(sent, live, to_near)
    cols, held, lent = lax.optimization_barrier((cols, held, lent))
    row_slot, crop_large, other_large, near_large, own_core, heads = live
    held = jnp.concatenate(
        [jnp.where(own_core == 0, held, lent), jnp.where(own_core == 0, lent, held)], axis=2
    )
    first, second = teacher_proj.shape[0], proj_large.shape[0]
    teacher_w = held[:, :first].reshape(-1, width)
    large_w = held[:, first : first + second].reshape(-1, width)
    huge_w = held[:, first + second : first + second + proj_huge.shape[0]].reshape(-1, width)
    teacher_cols = cols[:, :teacher_rows]
    student_cols = jnp.concatenate(
        [
            cols[:, teacher_rows:, : wide // near],
            cols[:, teacher_rows:, piece // 2 : piece // 2 + wide // near],
        ],
        axis=1,
    )
    near_large = near_large[:, None, None]
    zero = jnp.zeros((), jnp.bfloat16)
    part_teacher = jnp.einsum(
        "crf,fb->crb", teacher_cols, teacher_w, preferred_element_type=jnp.float32
    )
    part_student = jnp.einsum(
        "crf,fb->crb",
        jnp.where(near_large, student_cols[:, :, : large_w.shape[0]], zero),
        large_w,
        preferred_element_type=jnp.float32,
    ) + jnp.einsum(
        "crf,fb->crb",
        jnp.where(near_large, zero, student_cols),
        huge_w,
        preferred_element_type=jnp.float32,
    )
    live = (row_slot, crop_large, other_large, own_core, heads)
    parts, live = alone(jnp.concatenate([part_teacher, part_student], axis=1), live, to_near)
    units = unit_rows(jnp.sum(parts, axis=0))
    ring = tensors // halves
    rings = [[half * ring + place for place in range(ring)] for half in range(halves)]
    across = [[place, place + ring] for place in range(ring)]

    def to_ring(values):
        return lax.all_to_all(
            values, "tensor", split_axis=0, concat_axis=0, tiled=True, axis_index_groups=rings
        )

    def to_tensor(values):
        return lax.all_to_all(values, "tensor", split_axis=0, concat_axis=0, tiled=True)

    def to_half(values):
        return lax.all_gather(values, "tensor", axis=0, tiled=True, axis_index_groups=across)

    units, live = alone(jnp.broadcast_to(units[None], (ring, *units.shape)), live, to_ring)
    units, live = alone(units, live, to_half)
    row_slot, crop_large, other_large, own_core, heads = live
    teacher_proto, center, proto_large, proto_huge = heads
    chosen = (
        row_slot[:, None] == jnp.arange(tensors * PATCH, dtype=jnp.int32)[None, :]
    ).astype(jnp.bfloat16)
    kept_rows = crop_large == (own_core == 0)
    other_rows = other_large == (own_core == 0)
    teacher_units = units[:, :teacher_rows].reshape(-1, width)
    slot_units = units[:, teacher_rows:].reshape(-1, width)

    student_units = jnp.dot(chosen, slot_units, preferred_element_type=jnp.float32).astype(
        jnp.bfloat16
    )
    both_units = jnp.concatenate(
        [jnp.where(crop_large, student_units, zero), jnp.where(crop_large, zero, student_units)],
        axis=1,
    )
    both_protos = jnp.concatenate([proto_large, proto_huge], axis=0)
    shifted = (
        jnp.dot(teacher_units, teacher_proto, preferred_element_type=jnp.float32) - center[None, :]
    ) / TEACHER_TEMP
    scores = jnp.dot(both_units, both_protos, preferred_element_type=jnp.float32) / STUDENT_TEMP

    teacher_top = jnp.max(shifted, axis=1)
    teacher_exp = jnp.exp(shifted - teacher_top[:, None])
    teacher_sum = jnp.sum(teacher_exp, axis=1)
    student_top = jnp.max(scores, axis=1)
    student_sum = jnp.sum(jnp.exp(scores - student_top[:, None]), axis=1)
    stats = jnp.stack(
        [
            teacher_top + jnp.log(teacher_sum),
            jnp.sum(teacher_exp * scores, axis=1) / teacher_sum,
            student_top + jnp.log(student_sum),
        ]
    )
    stats = jnp.broadcast_to(stats.reshape(1, -1, 128), (tensors, stats.size // 128, 128))
    live = (shifted, scores, student_units, kept_rows, other_rows, own_core)
    stats, live = alone(stats, live, to_tensor)
    shifted, scores, student_units, kept_rows, other_rows, own_core = live
    stats = stats.reshape(tensors, 3, -1)
    log_t = log_total(stats[:, 0])
    crossed = jnp.sum(stats[:, 1] * jnp.exp(stats[:, 0] - log_t[None, :]), axis=0)
    log_s = log_total(stats[:, 2])
    group_loss = jnp.sum((log_s - crossed).reshape(-1, 128), axis=0)
    target = lax.reduce_precision(jnp.exp(shifted - log_t[:, None]), 8, 7)
    student_prob = jnp.exp(scores - log_s[:, None])
    deltas = ((student_prob - target) / STUDENT_TEMP).astype(jnp.bfloat16)

    rows = deltas.shape[0]
    note = jnp.pad(parts_of(group_loss), ((0, PATCH - 3), (0, protos + width - 128)))
    got = lax.ppermute(
        jnp.concatenate([jnp.concatenate([deltas, student_units], axis=1), note], axis=0),
        "group",
        pairs,
    )
    chip_grad = partial_grad(jnp.where(kept_rows, student_units, zero), deltas) + partial_grad(
        jnp.where(other_rows, got[:rows, protos:], zero), got[:rows, :protos]
    )
    chip_loss = group_loss + jnp.sum(got[rows : rows + 3, :128].astype(jnp.float32), axis=0)
    chips = groups // 2
    grad_rows = width // chips
    note = jnp.pad(parts_of(chip_loss), ((0, grad_rows - 3), (0, 0)))
    sent = jnp.concatenate(
        [
            chip_grad.astype(jnp.bfloat16).reshape(chips, grad_rows, protos),
            jnp.broadcast_to(note[None], (chips, grad_rows, 128)),
        ],
        axis=2,
    )
    same_core = [[core + 2 * chip for chip in range(chips)] for core in range(2)]
    taken = lax.all_to_all(
        sent, "group", split_axis=0, concat_axis=0, tiled=True, axis_index_groups=same_core
    )
    loss = (
        jnp.sum(taken[:, :3, protos:].astype(jnp.float32)) / (routes.shape[0] * PATCH)
    ).reshape(1)
    summed = jnp.sum(taken[:, :, :protos].astype(jnp.float32), axis=0) / PATCH
    mine = lax.all_to_all(
        jnp.broadcast_to(summed.astype(jnp.bfloat16)[None], (chips, grad_rows, protos)),
        "group",
        split_axis=0,
        concat_axis=0,
        tiled=True,
        axis_index_groups=same_core,
    ).reshape(width, protos)
    other = lax.ppermute(mine, "group", pairs)
    return (
        loss,
        jnp.where(own_core == 0, mine, other),
        jnp.where(own_core == 0, other, mine),
    )


def solution(mesh):
    placed = (
        P(("group", "tensor"), None),
        P(),
        P("tensor", None),
        P(None, "tensor"),
        P("tensor"),
        P(),
        P(),
        P(("group", "tensor"), None),
        P(("group", "tensor"), None),
        P(),
        P(),
        P("tensor", None),
        P("tensor", None),
        P(None, "tensor"),
        P(None, "tensor"),
    )
    return jax.shard_map(
        shards,
        mesh=mesh,
        in_specs=placed,
        out_specs=(P(), P(None, "tensor"), P(None, "tensor")),
        check_vma=False,
    )
```

```python
import jax
import jax.numpy as jnp
from jax import lax
from jax.experimental import pallas as pl
from jax.experimental.pallas import tpu as pltpu
from jax.sharding import PartitionSpec as P

PATCH = 16
CG = 16
FAR = 4


TEACHER_TEMP = 0.07
STUDENT_TEMP = 0.1
EPSILON = 1e-06


def unit_rows(middle):
    return (middle * lax.rsqrt(jnp.mean(middle * middle, axis=-1, keepdims=True) + EPSILON)).astype(
        jnp.bfloat16
    )


def gather_copies(values, axis):
    copies = jnp.broadcast_to(values[None], (lax.axis_size(axis), *values.shape))
    return lax.all_to_all(copies, axis, split_axis=0, concat_axis=0, tiled=True)


def log_total(logs):
    top = jnp.max(logs, axis=0)
    return top + jnp.log(jnp.sum(jnp.exp(logs - top[None, :]), axis=0))


def parts_of(values):
    high = lax.reduce_precision(values, 8, 7)
    middle = lax.reduce_precision(values - high, 8, 7)
    low = lax.reduce_precision(values - high - middle, 8, 7)
    return jnp.stack([high, middle, low]).astype(jnp.bfloat16)


def crop_rows(routes, group, large, own_places):
    target_group = lax.dynamic_index_in_dim(routes[:, 0].reshape(-1, CG), group, 0, keepdims=False)
    earlier = jnp.arange(CG)[:, None] > jnp.arange(CG)[None, :]
    matching = target_group[:, None] == target_group[None, :]
    slot_rank = jnp.sum((matching & earlier).astype(jnp.int32), axis=1)
    slots = own_places.shape[0]
    crop_slot = target_group * (slots * CG // routes.shape[0]) + slot_rank
    named = crop_slot[:, None] == jnp.arange(slots, dtype=jnp.int32)[None, :]
    first_row = jnp.sum(jnp.where(named, own_places[None, :], 0), axis=1) * PATCH
    row_slot = (first_row[:, None] + jnp.arange(PATCH, dtype=jnp.int32)[None, :]).reshape(-1)
    return (row_slot, jnp.repeat(target_group < large, PATCH)[:, None])


def partial_grad(units, deltas):
    return lax.dot_general(
        units, deltas, (((0,), (0,)), ((), ())), preferred_element_type=jnp.float32
    )


def alone(values, live, exchange):
    values, live = lax.optimization_barrier((values, live))
    return lax.optimization_barrier((exchange(values), live))


def around(first, second, count):
    return min((first - second) % count, (second - first) % count)


def hops(first_group, first_tensor, second_group, second_tensor):
    first_x = first_group // 8 * 2 + first_tensor // 16
    second_x = second_group // 8 * 2 + second_tensor // 16
    return (
        around(first_x, second_x, 4)
        + around(first_group // 2, second_group // 2, 4)
        + around(first_tensor, second_tensor, 16)
    )


def best_places(costs):
    count = len(costs)
    rows, cols, match = [0] * (count + 1), [0] * (count + 1), [0] * (count + 1)
    for row in range(1, count + 1):
        match[0], col = row, 0
        least, back, used = [1 << 60] * (count + 1), [0] * (count + 1), [False] * (count + 1)
        while match[col]:
            used[col] = True
            current, step, following = match[col], 1 << 60, 0
            for other in range(1, count + 1):
                if not used[other]:
                    left = costs[current - 1][other - 1] - rows[current] - cols[other]
                    if left < least[other]:
                        least[other], back[other] = left, col
                    if least[other] < step:
                        step, following = least[other], other
            for other in range(count + 1):
                if used[other]:
                    rows[match[other]] += step
                    cols[other] -= step
                else:
                    least[other] -= step
            col = following
        while col:
            match[col] = match[back[col]]
            col = back[col]
    places = [0] * count
    for col in range(1, count + 1):
        places[match[col] - 1] = col - 1
    return places


def slot_places(groups, tensors):
    slots_per = tensors // groups
    return [
        best_places(
            [
                [hops(slot // slots_per, s * slots_per + slot % slots_per, s, t) ** 6 for t in range(tensors)]
                for slot in range(tensors)
            ]
        )
        for s in range(groups)
    ]


def normed_rows(values, gains):
    row_mean = jnp.mean(values, axis=-1, keepdims=True)
    centred = values - row_mean
    spread = jnp.mean(centred * centred, axis=-1, keepdims=True)
    return centred * lax.rsqrt(spread + EPSILON) * gains


def near_columns(values, tensors, dest):
    wide = values.shape[1] // tensors
    half, low = dest // FAR, dest % FAR
    places = [(half * FAR + place) * FAR + low for place in range(FAR)]
    return [values[:, place * wide : (place + 1) * wide] for place in places]


def prepare_kernel(
    teacher_w, large_w, huge_w, teacher_x, gain, weights, sent
):
    own_group = lax.axis_index("group")
    half = weights.shape[2]
    first, second, third = teacher_w.shape[0], large_w.shape[0], huge_w.shape[0]
    low_core = lax.rem(own_group, 2) == 0
    spare = weights.shape[1] - first - second - third
    end = jnp.concatenate([huge_w[...], jnp.zeros((spare, 2 * half), huge_w.dtype)], axis=0)
    for start, rows in ((0, teacher_w[...]), (first, large_w[...]), (first + second, end)):
        kept = jnp.where(low_core, rows[:, :half], rows[:, half:])
        for place in range(FAR):
            weights[place, start : start + rows.shape[0], :] = kept
    normed = normed_rows(teacher_x[...].astype(jnp.float32), gain[...]).astype(jnp.bfloat16)
    tensors = sent.shape[0] * FAR
    for dest in range(sent.shape[0]):
        sent[dest] = jnp.concatenate(near_columns(normed, tensors, dest), axis=1)


def prepare(teacher_w, large_w, huge_w, teacher_x, gain, near):
    rows = teacher_w.shape[0] + large_w.shape[0] + huge_w.shape[0]
    rows += -rows % 16
    whole = pl.BlockSpec(memory_space=pltpu.VMEM)
    return pl.pallas_call(
        prepare_kernel,
        out_shape=(
            jax.ShapeDtypeStruct((FAR, rows, teacher_w.shape[1] // 2), jnp.bfloat16),
            jax.ShapeDtypeStruct((near, teacher_x.shape[0], teacher_x.shape[1] // near), jnp.bfloat16),
        ),
        in_specs=[whole] * 5,
        out_specs=(whole, whole),
    )(teacher_w, large_w, huge_w, teacher_x, gain.reshape(1, -1))


def student_kernel(large_groups, owners, student, gain_large, gain_huge, teacher, sent):
    own_group, own_tensor = lax.axis_index("group"), lax.axis_index("tensor")
    groups, tensors = owners.shape
    is_large = owners[own_group, own_tensor] // (tensors // groups) < large_groups[0]
    rows = teacher.shape[1]

    def send(normed):
        for dest in range(sent.shape[0]):
            columns = near_columns(normed, tensors, dest)
            filled = FAR * columns[0].shape[1]
            columns.append(jnp.zeros((2 * rows, sent.shape[2] // 2 - filled), jnp.float32))
            block = jnp.concatenate(columns, axis=1)
            block = jnp.concatenate([block[:rows], block[rows:]], axis=1)
            block = jnp.concatenate([teacher[dest].astype(jnp.float32), block], axis=0)
            sent[dest] = block.astype(jnp.bfloat16)

    @pl.when(is_large)
    def _():
        send(normed_rows(student[:, : gain_large.shape[1]].astype(jnp.float32), gain_large[...]))

    @pl.when(jnp.logical_not(is_large))
    def _():
        send(normed_rows(student[...].astype(jnp.float32), gain_huge[...]))


def student_columns(large_groups, owners, student, gain_large, gain_huge, teacher):
    near, rows, wide = teacher.shape
    whole = pl.BlockSpec(memory_space=pltpu.VMEM)
    scalars = pl.BlockSpec(memory_space=pltpu.SMEM)
    return pl.pallas_call(
        student_kernel,
        out_shape=jax.ShapeDtypeStruct((near, 2 * rows, wide), jnp.bfloat16),
        in_specs=[scalars, scalars] + [whole] * 4,
        out_specs=whole,
    )(large_groups, owners, student, gain_large.reshape(1, -1), gain_huge.reshape(1, -1), teacher)


def shards(
    teacher_feat,
    teacher_gain,
    teacher_proj,
    teacher_proto,
    center,
    routes,
    large_groups,
    feat_large,
    feat_huge,
    gain_large,
    gain_huge,
    proj_large,
    proj_huge,
    proto_large,
    proto_huge,
):
    groups = lax.axis_size("group")
    tensors = lax.axis_size("tensor")
    own_group = lax.axis_index("group")
    own_tensor = lax.axis_index("tensor")
    protos = teacher_proto.shape[1]
    width = teacher_proto.shape[0]
    slots_per = tensors // groups
    near = tensors // FAR
    halves = tensors // (FAR * FAR)
    own_far = own_tensor // FAR % FAR
    own_core = own_group % 2
    near_groups = [
        [half * FAR * FAR + place * FAR + low for half in range(halves) for low in range(FAR)]
        for place in range(FAR)
    ]
    far_groups = [
        [half * FAR * FAR + place * FAR + low for place in range(FAR)]
        for half in range(halves)
        for low in range(FAR)
    ]
    pairs = [(g, g ^ 1) for g in range(groups)]

    padded_large = jnp.pad(feat_large, ((0, 0), (0, feat_huge.shape[1] - feat_large.shape[1])))
    student_feat = jnp.where(own_group < large_groups[0], padded_large, feat_huge)
    weights, teacher_sent = prepare(
        teacher_proj, proj_large, proj_huge, teacher_feat, teacher_gain, near
    )
    places = slot_places(groups, tensors)
    owners = [[row.index(place) for place in range(tensors)] for row in places]
    swap = [
        (j * tensors + s * slots_per + k, s * tensors + places[s][j * slots_per + k])
        for j in range(groups)
        for s in range(groups)
        for k in range(slots_per)
    ]
    student_feat = lax.ppermute(student_feat, ("group", "tensor"), swap)
    table = [[owners[g], places[g], places[g ^ 1]] for g in range(groups)]
    owners = jnp.array(owners, jnp.int32)
    table = lax.dynamic_index_in_dim(jnp.array(table, jnp.int32), own_group, 0, keepdims=False)
    large_places = table[0] // slots_per < large_groups[0]

    held = lax.all_to_all(
        weights,
        "tensor",
        split_axis=0,
        concat_axis=0,
        tiled=True,
        axis_index_groups=far_groups,
    )
    lent = lax.ppermute(held, "group", pairs)

    teacher_rows, wide = teacher_feat.shape[0], feat_huge.shape[1]
    piece = teacher_feat.shape[1] // near
    sent = student_columns(
        large_groups, owners, student_feat, gain_large, gain_huge, teacher_sent
    )

    def to_near(values):
        return lax.all_to_all(
            values,
            "tensor",
            split_axis=0,
            concat_axis=0,
            tiled=True,
            axis_index_groups=near_groups,
        )

    row_slot, crop_large = crop_rows(routes, own_group, large_groups[0], table[1])
    _, other_large = crop_rows(routes, own_group ^ 1, large_groups[0], table[2])
    near_large = lax.dynamic_index_in_dim(
        large_places.reshape(halves, FAR, FAR), own_far, 1, keepdims=False
    ).reshape(-1)
    heads = (teacher_proto, center, proto_large, proto_huge)
    live = (row_slot, crop_large, other_large, near_large, own_core, heads)
    cols, live = alone(sent, live, to_near)
    cols, held, lent = lax.optimization_barrier((cols, held, lent))
    row_slot, crop_large, other_large, near_large, own_core, heads = live
    held = jnp.concatenate(
        [jnp.where(own_core == 0, held, lent), jnp.where(own_core == 0, lent, held)], axis=2
    )
    first, second = teacher_proj.shape[0], proj_large.shape[0]
    teacher_w = held[:, :first].reshape(-1, width)
    large_w = held[:, first : first + second].reshape(-1, width)
    huge_w = held[:, first + second : first + second + proj_huge.shape[0]].reshape(-1, width)
    teacher_cols = cols[:, :teacher_rows]
    student_cols = jnp.concatenate(
        [
            cols[:, teacher_rows:, : wide // near],
            cols[:, teacher_rows:, piece // 2 : piece // 2 + wide // near],
        ],
        axis=1,
    )
    near_large = near_large[:, None, None]
    zero = jnp.zeros((), jnp.bfloat16)
    part_teacher = jnp.einsum(
        "crf,fb->crb", teacher_cols, teacher_w, preferred_element_type=jnp.float32
    )
    part_student = jnp.einsum(
        "crf,fb->crb",
        jnp.where(near_large, student_cols[:, :, : large_w.shape[0]], zero),
        large_w,
        preferred_element_type=jnp.float32,
    ) + jnp.einsum(
        "crf,fb->crb",
        jnp.where(near_large, zero, student_cols),
        huge_w,
        preferred_element_type=jnp.float32,
    )
    live = (row_slot, crop_large, other_large, own_core, heads)
    parts, live = alone(jnp.concatenate([part_teacher, part_student], axis=1), live, to_near)
    units = unit_rows(jnp.sum(parts, axis=0))
    ring = tensors // halves
    rings = [[half * ring + place for place in range(ring)] for half in range(halves)]
    across = [[place, place + ring] for place in range(ring)]

    def to_ring(values):
        return lax.all_to_all(
            values, "tensor", split_axis=0, concat_axis=0, tiled=True, axis_index_groups=rings
        )

    def to_tensor(values):
        return lax.all_to_all(values, "tensor", split_axis=0, concat_axis=0, tiled=True)

    def to_half(values):
        return lax.all_gather(values, "tensor", axis=0, tiled=True, axis_index_groups=across)

    units, live = alone(jnp.broadcast_to(units[None], (ring, *units.shape)), live, to_ring)
    units, live = alone(units, live, to_half)
    row_slot, crop_large, other_large, own_core, heads = live
    teacher_proto, center, proto_large, proto_huge = heads
    chosen = (
        row_slot[:, None] == jnp.arange(tensors * PATCH, dtype=jnp.int32)[None, :]
    ).astype(jnp.bfloat16)
    kept_rows = crop_large == (own_core == 0)
    other_rows = other_large == (own_core == 0)
    teacher_units = units[:, :teacher_rows].reshape(-1, width)
    slot_units = units[:, teacher_rows:].reshape(-1, width)

    student_units = jnp.dot(chosen, slot_units, preferred_element_type=jnp.float32).astype(
        jnp.bfloat16
    )
    both_units = jnp.concatenate(
        [jnp.where(crop_large, student_units, zero), jnp.where(crop_large, zero, student_units)],
        axis=1,
    )
    both_protos = jnp.concatenate([proto_large, proto_huge], axis=0)
    shifted = (
        jnp.dot(teacher_units, teacher_proto, preferred_element_type=jnp.float32) - center[None, :]
    ) / TEACHER_TEMP
    scores = jnp.dot(both_units, both_protos, preferred_element_type=jnp.float32) / STUDENT_TEMP

    teacher_top = jnp.max(shifted, axis=1)
    teacher_exp = jnp.exp(shifted - teacher_top[:, None])
    teacher_sum = jnp.sum(teacher_exp, axis=1)
    student_top = jnp.max(scores, axis=1)
    student_sum = jnp.sum(jnp.exp(scores - student_top[:, None]), axis=1)
    stats = jnp.stack(
        [
            teacher_top + jnp.log(teacher_sum),
            jnp.sum(teacher_exp * scores, axis=1) / teacher_sum,
            student_top + jnp.log(student_sum),
        ]
    )
    stats = jnp.broadcast_to(stats[None], (tensors, *stats.shape))
    live = (shifted, scores, student_units, kept_rows, other_rows, own_core)
    stats, live = alone(stats, live, to_tensor)
    shifted, scores, student_units, kept_rows, other_rows, own_core = live
    stats = stats.reshape(tensors, 3, -1)
    log_t = log_total(stats[:, 0])
    crossed = jnp.sum(stats[:, 1] * jnp.exp(stats[:, 0] - log_t[None, :]), axis=0)
    log_s = log_total(stats[:, 2])
    group_loss = jnp.sum((log_s - crossed).reshape(-1, 128), axis=0)
    target = lax.reduce_precision(jnp.exp(shifted - log_t[:, None]), 8, 7)
    student_prob = jnp.exp(scores - log_s[:, None])
    deltas = ((student_prob - target) / STUDENT_TEMP).astype(jnp.bfloat16)

    rows = deltas.shape[0]
    note = jnp.pad(parts_of(group_loss), ((0, PATCH - 3), (0, protos + width - 128)))
    got = lax.ppermute(
        jnp.concatenate([jnp.concatenate([deltas, student_units], axis=1), note], axis=0),
        "group",
        pairs,
    )
    chip_grad = partial_grad(jnp.where(kept_rows, student_units, zero), deltas) + partial_grad(
        jnp.where(other_rows, got[:rows, protos:], zero), got[:rows, :protos]
    )
    chip_loss = group_loss + jnp.sum(got[rows : rows + 3, :128].astype(jnp.float32), axis=0)
    chips = groups // 2
    grad_rows = width // chips
    note = jnp.pad(parts_of(chip_loss), ((0, grad_rows - 3), (0, 0)))
    sent = jnp.concatenate(
        [
            chip_grad.astype(jnp.bfloat16).reshape(chips, grad_rows, protos),
            jnp.broadcast_to(note[None], (chips, grad_rows, 128)),
        ],
        axis=2,
    )
    same_core = [[core + 2 * chip for chip in range(chips)] for core in range(2)]
    taken = lax.all_to_all(
        sent, "group", split_axis=0, concat_axis=0, tiled=True, axis_index_groups=same_core
    )
    loss = (
        jnp.sum(taken[:, :3, protos:].astype(jnp.float32)) / (routes.shape[0] * PATCH)
    ).reshape(1)
    summed = jnp.sum(taken[:, :, :protos].astype(jnp.float32), axis=0) / PATCH
    mine = lax.all_to_all(
        jnp.broadcast_to(summed.astype(jnp.bfloat16)[None], (chips, grad_rows, protos)),
        "group",
        split_axis=0,
        concat_axis=0,
        tiled=True,
        axis_index_groups=same_core,
    ).reshape(width, protos)
    other = lax.ppermute(mine, "group", pairs)
    return (
        loss,
        jnp.where(own_core == 0, mine, other),
        jnp.where(own_core == 0, other, mine),
    )


def solution(mesh):
    placed = (
        P(("group", "tensor"), None),
        P(),
        P("tensor", None),
        P(None, "tensor"),
        P("tensor"),
        P(),
        P(),
        P(("group", "tensor"), None),
        P(("group", "tensor"), None),
        P(),
        P(),
        P("tensor", None),
        P("tensor", None),
        P(None, "tensor"),
        P(None, "tensor"),
    )
    return jax.shard_map(
        shards,
        mesh=mesh,
        in_specs=placed,
        out_specs=(P(), P(None, "tensor"), P(None, "tensor")),
        check_vma=False,
    )
```
